128 devices in a mesh: row: 16 (over z, x_hi, core), col: 8 (over x_lo, y).
Axes of the slice: x: 4 (x_hi: 2, x_lo: 2; x = x_hi * 2 + x_lo), y: 4, z: 4, core: 2. Of those that a mesh axis runs over, the one named last changes fastest.
Arguments:
- vectors: bfloat16 [256, 64, 128], P(('col', 'row')), may hold values from -6 to 6
- b1_rows: int32 [16, 8, 32], P('row', 'col'), may hold values from 0 to 7, as said below
- b1_cols: int32 [16, 8, 32], P('row', 'col'), may hold values from 0 to 31, as said below
- b1_count: int32 [16, 8], P('row', 'col'), may hold values from 16 to 32, as said below
- b1_values: bfloat16 [16, 8, 32, 128, 128], P('row', 'col'), may hold values from -1 to 1, as said below
- b2_rows: int32 [16, 8, 256], P('row', 'col'), may hold values from 0 to 31, as said below
- b2_cols: int32 [16, 8, 256], P('row', 'col'), may hold values from 0 to 63, as said below
- b2_count: int32 [16, 8], P('row', 'col'), may hold values from 128 to 256, as said below
- b2_values: bfloat16 [16, 8, 256, 128, 128], P('row', 'col'), may hold values from -1 to 1, as said below
Outputs:
- subspace: float32 [256, 64, 128], P(('col', 'row'))
The draws below stay inside these ranges and needn't reach their ends.
Inputs may be any that keep to these rules, and one draw needn't show every extreme that they name: `b1_rows`: row block within the device's row range; the (row, column) pairs of one device's list are distinct; slots at or past that device's count are ignored. `b1_cols`: unknown block within the device's column range. `b1_count`: one device in every draw uses all 32 slots. `b1_values`: every entry is +1 or -1. `b2_rows`: unknown block within the device's column range; the (row, column) pairs of one device's list are distinct; slots at or past that device's count are ignored. `b2_cols`: column block within the device's row range. `b2_count`: one device in every draw uses all 256 slots. `b2_values`: every entry is +1 or -1.
All inputs are finite; a program needn't handle non-finite values.
Results may differ from the reference program's by a relative error of at most 0.01.
Values may be sent and summed in bfloat16 or wider, within the bound.
A program may use at most 128 MiB of HBM per device.

```python
import jax
import jax.numpy as jnp
from jax import lax

BLOCK = 128
K = 64
APPS = 3
NB1 = 32
NB2 = 256
VB_ROW = 8
TB_ROW = 64
EB_COL = 32
EDGE_BLOCKS = 256
NORM = 18432
N_ROW = 16
N_COL = 8


def block_positions(key, marker, listed, height, across):
    subkey = jax.random.fold_in(key, marker)
    positions = height * across
    ceiling = max(2 ** 30 // positions, 2)
    scores = jax.random.randint(subkey, (N_ROW, N_COL, positions), 0, ceiling) * positions + jnp.arange(positions, dtype=jnp.int32)
    ordering = jnp.argsort(scores, axis=-1)[..., :listed].astype(jnp.int32)
    return (ordering // across, ordering % across)


def counts_for(key, marker, listed):
    subkey = jax.random.fold_in(key, marker)
    split_one, split_two = jax.random.split(subkey)
    counts = jax.random.randint(split_one, (N_ROW * N_COL,), listed // 2, listed + 1)
    busiest = jax.random.randint(split_two, (), 0, N_ROW * N_COL)
    flattened = jnp.where(jnp.arange(N_ROW * N_COL, dtype=jnp.int32) == busiest, listed, counts)
    return flattened.reshape(N_ROW, N_COL).astype(jnp.int32)


def draw_b1_rows(key, part):
    return block_positions(key, 11, NB1, VB_ROW, EB_COL)[0]


def draw_b1_cols(key, part):
    return block_positions(key, 11, NB1, VB_ROW, EB_COL)[1]


def draw_b1_count(key, part):
    return counts_for(key, 21, NB1)


def draw_b1_values(key, part):
    signs = jax.random.rademacher(jax.random.fold_in(key, 31), (N_ROW, N_COL, NB1, BLOCK, BLOCK), dtype=jnp.float32)
    return signs.astype(jnp.bfloat16)


def draw_b2_rows(key, part):
    return block_positions(key, 12, NB2, EB_COL, TB_ROW)[0]


def draw_b2_cols(key, part):
    return block_positions(key, 12, NB2, EB_COL, TB_ROW)[1]


def draw_b2_count(key, part):
    return counts_for(key, 22, NB2)


def draw_b2_values(key, part):
    signs = jax.random.rademacher(jax.random.fold_in(key, 32), (N_ROW, N_COL, NB2, BLOCK, BLOCK), dtype=jnp.float32)
    return signs.astype(jnp.bfloat16)


def level_of(stream_key, shape, cuts, least, high):
    level = 1.0
    for position, parts in cuts:
        heights = jax.random.uniform(jax.random.fold_in(jax.random.fold_in(stream_key, 6), position), (parts,), jnp.float32, least / len(cuts), high / len(cuts))
        level = level * jnp.repeat(jnp.exp(heights), shape[position] // parts).reshape((-1,) + (1,) * (len(shape) - 1 - position))
    return level


def scatter_about(key, dims, width, most, cuts=(), kind=jnp.bfloat16):
    loudness = level_of(key, dims, cuts, -0.22, 0.18) if cuts else 1.0
    drawn = jax.random.normal(key, dims, jnp.float32) * width * loudness
    return jnp.minimum(jnp.maximum(drawn, -most), most).astype(kind)


def setup_inputs(seed: int = 0) -> dict:
    seeds = jax.random.split(jax.random.key(seed), 10)
    return {
        "vectors": scatter_about(seeds[0], (EDGE_BLOCKS, K, BLOCK), 1.0, 6.0, ((0, 128),)),
        "b1_rows": draw_b1_rows(jax.random.fold_in(seeds[9], 71), 0),
        "b1_cols": draw_b1_cols(jax.random.fold_in(seeds[9], 71), 0),
        "b1_count": draw_b1_count(jax.random.fold_in(seeds[9], 71), 0),
        "b1_values": draw_b1_values(jax.random.fold_in(seeds[9], 71), 0),
        "b2_rows": draw_b2_rows(jax.random.fold_in(seeds[9], 71), 0),
        "b2_cols": draw_b2_cols(jax.random.fold_in(seeds[9], 71), 0),
        "b2_count": draw_b2_count(jax.random.fold_in(seeds[9], 71), 0),
        "b2_values": draw_b2_values(jax.random.fold_in(seeds[9], 71), 0),
    }


def apply_blocks(values, block_rows, block_cols, filled, source, segments, transpose):
    active = (jnp.arange(values.shape[0], dtype=jnp.int32) < filled).astype(jnp.float32)
    wide = values.astype(jnp.float32)
    if transpose:
        picked = source[block_rows].astype(jnp.float32)
        products = jnp.einsum("bji,bkj->bki", wide, picked)
        target = block_cols
    else:
        picked = source[block_cols].astype(jnp.float32)
        products = jnp.einsum("bij,bkj->bki", wide, picked)
        target = block_rows
    return jax.ops.segment_sum(products * active[:, None, None], target, num_segments=segments)


def reference(vectors, b1_rows, b1_cols, b1_count, b1_values, b2_rows, b2_cols, b2_count, b2_values):
    current = vectors
    scaled = vectors.astype(jnp.float32)
    for repeat in range(APPS):
        edge_sets = current.reshape(N_COL, EB_COL, K, BLOCK)

        def faces_of_row(row_index):
            def add_col(totals, col_index):
                source = edge_sets[col_index]
                vertex_total = totals[0] + apply_blocks(b1_values[row_index, col_index], b1_rows[row_index, col_index], b1_cols[row_index, col_index], b1_count[row_index, col_index], source, VB_ROW, False)
                triangle_total = totals[1] + apply_blocks(b2_values[row_index, col_index], b2_rows[row_index, col_index], b2_cols[row_index, col_index], b2_count[row_index, col_index], source, TB_ROW, True)
                return (vertex_total, triangle_total), None

            start_totals = (jnp.zeros((VB_ROW, K, BLOCK), jnp.float32), jnp.zeros((TB_ROW, K, BLOCK), jnp.float32))
            totals, unused = lax.scan(add_col, start_totals, jnp.arange(N_COL, dtype=jnp.int32))
            return totals[0].astype(jnp.bfloat16), totals[1].astype(jnp.bfloat16)

        vertex_half, triangle_half = lax.map(faces_of_row, jnp.arange(N_ROW, dtype=jnp.int32))

        def edges_of_col(col_index):
            def add_row(total, row_index):
                total = total + apply_blocks(b1_values[row_index, col_index], b1_rows[row_index, col_index], b1_cols[row_index, col_index], b1_count[row_index, col_index], vertex_half[row_index], EB_COL, True)
                total = total + apply_blocks(b2_values[row_index, col_index], b2_rows[row_index, col_index], b2_cols[row_index, col_index], b2_count[row_index, col_index], triangle_half[row_index], EB_COL, False)
                return total, None

            total, unused = lax.scan(add_row, jnp.zeros((EB_COL, K, BLOCK), jnp.float32), jnp.arange(N_ROW, dtype=jnp.int32))
            return total

        edge_total = lax.map(edges_of_col, jnp.arange(N_COL, dtype=jnp.int32)).reshape(EDGE_BLOCKS, K, BLOCK)
        scaled = edge_total * (1.0 / NORM)
        current = scaled.astype(jnp.bfloat16)
    return scaled
```

```python
import functools

import jax
import jax.numpy as jnp
from jax import lax
from jax.experimental import pallas as pl
from jax.experimental.pallas import tpu as pltpu
from jax.sharding import PartitionSpec as P

BLOCK = 128
K = 64
APPS = 3
NB1 = 32
NB2 = 256
VB_ROW = 8
TB_ROW = 64
EB_COL = 32
NORM = 18432
N_ROW = 16
N_COL = 8
OWN = EB_COL // N_ROW
FACES = 1 + TB_ROW // N_COL
UNROLL = 8
MESH = pl.DeviceIdType.MESH
F32 = jnp.float32
BF16 = jnp.bfloat16

FC, FA, BC, BA = range(4)


def plan_kernel(counts, b1_rows, b1_cols, b2_rows, b2_cols, ints, floats):
    def plan(which, target, source, filled, segments):
        n = target.shape[1]
        lanes = lax.broadcasted_iota(jnp.int32, (n, n), 1)
        rows = lax.broadcasted_iota(jnp.int32, (n, n), 0)
        place = lax.broadcasted_iota(jnp.int32, (1, n), 1)
        target = jnp.where(place < filled, target, segments)
        key = target * n + place

        def column(line):
            return jnp.sum(jnp.where(rows == lanes, line, 0), axis=1, keepdims=True)

        rank = jnp.sum(jnp.where(key < column(key), 1, 0), axis=1, keepdims=True)
        hit = rank == lanes
        follows = (rank + 1) == lanes

        def ordered(line, mask):
            return jnp.sum(jnp.where(mask, column(line), 0), axis=0, keepdims=True)

        here = ordered(target, hit)
        before = ordered(target + 1, follows) - 1
        slots = jnp.where(rank >= 0, rows, 0)
        ints[3 * which : 3 * which + 1, :n] = jnp.sum(jnp.where(hit, slots, 0), axis=0, keepdims=True)
        ints[3 * which + 1 : 3 * which + 2, :n] = ordered(source, hit)
        floats[2 * which : 2 * which + 1, :n] = jnp.where(here == before, 1.0, 0.0)
        wide = 128
        segment = lax.broadcasted_iota(jnp.int32, (n, wide), 1)
        upright = column(target)
        end = jnp.sum(jnp.where(upright <= segment, 1, 0), axis=0, keepdims=True)
        start = jnp.sum(jnp.where(upright < segment, 1, 0), axis=0, keepdims=True)
        ints[3 * which + 2 : 3 * which + 3, :wide] = jnp.maximum(end - 1, 0)
        floats[2 * which + 1 : 2 * which + 2, :wide] = jnp.where(end > start, 1.0, 0.0)

    ints[...] = jnp.zeros_like(ints)
    floats[...] = jnp.zeros_like(floats)
    rows1, cols1, rows2, cols2 = b1_rows[...], b1_cols[...], b2_rows[...], b2_cols[...]
    per = TB_ROW // N_COL
    plan(FC, cols2, rows2, counts[1], TB_ROW)
    plan(FA, rows1, cols1, counts[0], VB_ROW)
    plan(BC, rows2, (cols2 // per) * FACES + 1 + cols2 % per, counts[1], EB_COL)
    plan(BA, cols1, rows1 * FACES, counts[0], EB_COL)


def make_plans(counts, b1_rows, b1_cols, b2_rows, b2_cols):
    return pl.pallas_call(
        plan_kernel,
        out_shape=(
            jax.ShapeDtypeStruct((12, NB2), jnp.int32),
            jax.ShapeDtypeStruct((8, NB2), F32),
        ),
        in_specs=[pl.BlockSpec(memory_space=pltpu.SMEM)] + [pl.BlockSpec(memory_space=pltpu.VMEM)] * 4,
        out_specs=(pl.BlockSpec(memory_space=pltpu.VMEM),) * 2,
    )(counts, b1_rows, b1_cols, b2_rows, b2_cols)


def main_kernel(
    apps, compute, comm,
    ints, floats, vectors, b1_hbm, b2_hbm, out,
    b1, b2, x, sums_c, sums_a, part, part_in, faces, image, image_in,
    load_sem, g_send, g_recv, s_send, s_recv, a_send, a_recv, r_send, r_recv,
):
    row, col = lax.axis_index("row"), lax.axis_index("col")
    load1 = pltpu.make_async_copy(b1_hbm, b1, load_sem.at[0])
    load2 = pltpu.make_async_copy(b2_hbm, b2, load_sem.at[1])
    load1.start()
    load2.start()
    row_peers = [lax.rem(row + d, N_ROW) for d in range(1, N_ROW)]
    col_peers = [lax.rem(col + d, N_COL) for d in range(1, N_COL)]

    barrier = pltpu.get_barrier_semaphore()
    for peer in row_peers:
        pl.semaphore_signal(barrier, inc=1, device_id=(peer, col), device_id_type=MESH)
    for peer in col_peers:
        pl.semaphore_signal(barrier, inc=1, device_id=(row, peer), device_id_type=MESH)
    x[pl.ds(OWN * row, OWN)] = vectors[...]
    pl.semaphore_wait(barrier, N_ROW + N_COL - 2)

    def remote(src, dst, sends, recvs, at, device):
        return pltpu.make_async_remote_copy(
            src_ref=src, dst_ref=dst, send_sem=sends.at[at], recv_sem=recvs.at[at],
            device_id=device, device_id_type=MESH,
        )

    def exchange(copies):
        if not comm:
            return
        for copy in copies:
            copy.start()
        for copy in copies:
            copy.wait()

    def sweep(which, n, values, source, sums, turned):
        dims = (((1,), (1,)), ((), ())) if turned else (((1,), (0,)), ((), ()))

        def body(step, total):
            for u in range(UNROLL):
                at = step * UNROLL + u
                product = lax.dot_general(
                    source[ints[3 * which + 1, at]], values[ints[3 * which, at]], dims,
                    preferred_element_type=F32,
                )
                total = total * floats[2 * which, at] + product
                sums[at] = total
            return total

        if compute:
            lax.fori_loop(0, n // UNROLL, body, jnp.zeros((K, BLOCK), F32))

    def picked(which, sums, target):
        return sums[ints[3 * which + 2, target]] * floats[2 * which + 1, target]

    for app in range(apps):
        own = pl.ds(OWN * row, OWN)
        exchange([
            remote(x.at[own], x.at[own], g_send, g_recv, d, (peer, col))
            for d, peer in enumerate(row_peers)
        ])
        if app == 0:
            load1.wait()
            load2.wait()
        sweep(FA, NB1, b1, x, sums_a, True)
        sweep(FC, NB2, b2, x, sums_c, False)

        def hand_faces(m, carry):
            part[m, 0] = picked(FA, sums_a, m).astype(BF16)
            for b in range(FACES - 1):
                part[m, 1 + b] = picked(FC, sums_c, m * (FACES - 1) + b).astype(BF16)
            return carry

        if compute:
            lax.fori_loop(0, N_COL, hand_faces, 0)
        exchange([
            remote(part.at[peer], part_in.at[d], s_send, s_recv, d, (row, peer))
            for d, peer in enumerate(col_peers)
        ])

        def sum_faces(b, carry):
            total = part[col, b].astype(F32)
            for d in range(N_COL - 1):
                total = total + part_in[d, b].astype(F32)
            faces[col * FACES + b] = total.astype(BF16)
            return carry

        if compute:
            lax.fori_loop(0, FACES, sum_faces, 0)
        mine = pl.ds(FACES * col, FACES)
        exchange([
            remote(faces.at[mine], faces.at[mine], a_send, a_recv, d, (row, peer))
            for d, peer in enumerate(col_peers)
        ])
        sweep(BA, NB1, b1, faces, sums_a, False)
        sweep(BC, NB2, b2, faces, sums_c, True)

        def hand_image(m, carry):
            for b in range(OWN):
                t = m * OWN + b
                image[m, b] = (picked(BA, sums_a, t) + picked(BC, sums_c, t)).astype(BF16)
            return carry

        if compute:
            lax.fori_loop(0, N_ROW, hand_image, 0)
        exchange([
            remote(image.at[peer], image_in.at[d], r_send, r_recv, d, (peer, col))
            for d, peer in enumerate(row_peers)
        ])
        for b in range(OWN):
            total = image[row, b].astype(F32)
            for d in range(N_ROW - 1):
                total = total + image_in[d, b].astype(F32)
            total = total * (1.0 / NORM)
            if app == apps - 1:
                out[b] = total
            else:
                x[OWN * row + b] = total.astype(BF16)


def build(mesh, apps=APPS, compute=True, comm=True):
    def shards(vectors, b1_rows, b1_cols, b1_count, b1_values, b2_rows, b2_cols, b2_count, b2_values):
        counts = jnp.concatenate([b1_count[0], b2_count[0]])
        ints, floats = make_plans(counts, b1_rows[0], b1_cols[0], b2_rows[0], b2_cols[0])
        vmem = pl.BlockSpec(memory_space=pltpu.VMEM)
        smem = pl.BlockSpec(memory_space=pltpu.SMEM)
        hbm = pl.BlockSpec(memory_space=pl.ANY)
        dma = pltpu.SemaphoreType.DMA
        return pl.pallas_call(
            functools.partial(main_kernel, apps, compute, comm),
            out_shape=jax.ShapeDtypeStruct((OWN, K, BLOCK), F32),
            in_specs=[smem, smem, vmem, hbm, hbm],
            out_specs=vmem,
            scratch_shapes=[
                pltpu.VMEM((NB1, BLOCK, BLOCK), BF16),
                pltpu.VMEM((NB2, BLOCK, BLOCK), BF16),
                pltpu.VMEM((EB_COL, K, BLOCK), BF16),
                pltpu.VMEM((NB2, K, BLOCK), F32),
                pltpu.VMEM((NB1, K, BLOCK), F32),
                pltpu.VMEM((N_COL, FACES, K, BLOCK), BF16),
                pltpu.VMEM((N_COL - 1, FACES, K, BLOCK), BF16),
                pltpu.VMEM((N_COL * FACES, K, BLOCK), BF16),
                pltpu.VMEM((N_ROW, OWN, K, BLOCK), BF16),
                pltpu.VMEM((N_ROW - 1, OWN, K, BLOCK), BF16),
                dma((2,)),
                dma((N_ROW - 1,)), dma((N_ROW - 1,)),
                dma((N_COL - 1,)), dma((N_COL - 1,)),
                dma((N_COL - 1,)), dma((N_COL - 1,)),
                dma((N_ROW - 1,)), dma((N_ROW - 1,)),
            ],
            compiler_params=pltpu.CompilerParams(
                collective_id=0, has_side_effects=True, vmem_limit_bytes=48 * 2**20
            ),
        )(ints, floats, vectors, b1_values[0, 0], b2_values[0, 0])

    return jax.shard_map(
        shards,
        mesh=mesh,
        in_specs=(
            P(("col", "row"), None, None),
            P("row", "col", None),
            P("row", "col", None),
            P("row", "col"),
            P("row", "col", None, None, None),
            P("row", "col", None),
            P("row", "col", None),
            P("row", "col"),
            P("row", "col", None, None, None),
        ),
        out_specs=P(("col", "row"), None, None),
        check_vma=False,
    )


def solution(mesh):
    return build(mesh)
```

```python
import functools

import jax
import jax.numpy as jnp
from jax import lax
from jax.experimental import pallas as pl
from jax.experimental.pallas import tpu as pltpu
from jax.sharding import PartitionSpec as P

BLOCK = 128
K = 64
APPS = 3
NB1 = 32
NB2 = 256
VB_ROW = 8
TB_ROW = 64
EB_COL = 32
NORM = 18432
N_ROW = 16
N_COL = 8
OWN = EB_COL // N_ROW
FACES = 1 + TB_ROW // N_COL
UNROLL = 32
MESH = pl.DeviceIdType.MESH
F32 = jnp.float32
BF16 = jnp.bfloat16

FC, FA, BC, BA = range(4)


def plan_kernel(counts, b1_rows, b1_cols, b2_rows, b2_cols, ints, floats):
    def plan(which, target, source, filled, segments):
        n = target.shape[1]
        lanes = lax.broadcasted_iota(jnp.int32, (n, n), 1)
        rows = lax.broadcasted_iota(jnp.int32, (n, n), 0)
        place = lax.broadcasted_iota(jnp.int32, (1, n), 1)
        target = jnp.where(place < filled, target, segments)
        key = target * n + place

        def column(line):
            return jnp.sum(jnp.where(rows == lanes, line, 0), axis=1, keepdims=True)

        rank = jnp.sum(jnp.where(key < column(key), 1, 0), axis=1, keepdims=True)
        hit = rank == lanes
        follows = (rank + 1) == lanes

        def ordered(line, mask):
            return jnp.sum(jnp.where(mask, column(line), 0), axis=0, keepdims=True)

        here = ordered(target, hit)
        before = ordered(target + 1, follows) - 1
        slots = jnp.where(rank >= 0, rows, 0)
        ints[3 * which : 3 * which + 1, :n] = jnp.sum(jnp.where(hit, slots, 0), axis=0, keepdims=True)
        ints[3 * which + 1 : 3 * which + 2, :n] = ordered(source, hit)
        floats[2 * which : 2 * which + 1, :n] = jnp.where(here == before, 1.0, 0.0)
        wide = 128
        segment = lax.broadcasted_iota(jnp.int32, (n, wide), 1)
        upright = column(target)
        end = jnp.sum(jnp.where(upright <= segment, 1, 0), axis=0, keepdims=True)
        start = jnp.sum(jnp.where(upright < segment, 1, 0), axis=0, keepdims=True)
        ints[3 * which + 2 : 3 * which + 3, :wide] = jnp.maximum(end - 1, 0)
        floats[2 * which + 1 : 2 * which + 2, :wide] = jnp.where(end > start, 1.0, 0.0)

    ints[...] = jnp.zeros_like(ints)
    floats[...] = jnp.zeros_like(floats)
    rows1, cols1, rows2, cols2 = b1_rows[...], b1_cols[...], b2_rows[...], b2_cols[...]
    per = TB_ROW // N_COL
    plan(FC, cols2, rows2, counts[1], TB_ROW)
    plan(FA, rows1, cols1, counts[0], VB_ROW)
    plan(BC, rows2, (cols2 // per) * FACES + 1 + cols2 % per, counts[1], EB_COL)
    plan(BA, cols1, rows1 * FACES, counts[0], EB_COL)


def make_plans(counts, b1_rows, b1_cols, b2_rows, b2_cols):
    return pl.pallas_call(
        plan_kernel,
        out_shape=(
            jax.ShapeDtypeStruct((12, NB2), jnp.int32),
            jax.ShapeDtypeStruct((8, NB2), F32),
        ),
        in_specs=[pl.BlockSpec(memory_space=pltpu.SMEM)] + [pl.BlockSpec(memory_space=pltpu.VMEM)] * 4,
        out_specs=(pl.BlockSpec(memory_space=pltpu.VMEM),) * 2,
    )(counts, b1_rows, b1_cols, b2_rows, b2_cols)


def order_of(apps, parts):
    if parts == 1:
        return [(step, app, 0) for app in range(apps) for step in "YFSBQR"]
    order = []
    for app in range(apps):
        order.append(("Y", app, 0))
        if app:
            order.append(("R", app - 1, 1))
        order += [(step, app, h) for step, h in zip("FYFSSBQBRQ", (0, 1, 1, 0, 1, 0, 0, 1, 0, 1))]
    return order + [("R", apps - 1, 1)]


def main_kernel(
    apps, parts, compute, order,
    ints, floats, vectors, b1_hbm, b2_hbm, out,
    b1, b2, b1_turned, b2_turned, x, sums_c, sums_a, part, part_in, faces,
    kept, lent, lent_in, middle, middle_in,
    load_sem, g_send, g_recv, y_send, y_recv, s_send, s_recv, a_send, a_recv, q_send, q_recv, r_send, r_recv,
):
    row, col = lax.axis_index("row"), lax.axis_index("col")
    height = K // parts
    chip, core = row // 2, lax.rem(row, 2)
    z, xh = chip // 2, lax.rem(chip, 2)
    other = 2 * chip + 1 - core

    def chip_at(dz, dx):
        return lax.rem(z + dz, 4) * 2 + lax.rem(xh + dx, 2)

    steps = [(2, 1), (1, 1), (3, 1), (2, 0), (0, 1), (1, 0), (3, 0)]
    to_chips = [chip_at(dz, dx) for dz, dx in steps]
    from_chips = [chip_at(4 - dz, dx) for dz, dx in steps]
    xl, y = col // 4, lax.rem(col, 4)
    col_peers = [
        lax.rem(xl + dx, 2) * 4 + lax.rem(y + dy, 4) for dx, dy in [(1, 2), (1, 1), (1, 3), (0, 2), (1, 0), (0, 1), (0, 3)]
    ]
    n_chips = len(steps)

    load1 = pltpu.make_async_copy(b1_hbm, b1, load_sem.at[0])
    load2 = pltpu.make_async_copy(b2_hbm, b2, load_sem.at[1])
    load1.start()
    load2.start()
    barrier = pltpu.get_barrier_semaphore()
    for peer in to_chips:
        pl.semaphore_signal(barrier, inc=1, device_id=(2 * peer + core, col), device_id_type=MESH)
    for peer in col_peers:
        pl.semaphore_signal(barrier, inc=1, device_id=(row, peer), device_id_type=MESH)
    pl.semaphore_signal(barrier, inc=1, device_id=(other, col), device_id_type=MESH)
    for h in range(parts):
        x[h][pl.ds(OWN * row, OWN)] = vectors[:, h * height : (h + 1) * height, :]
    pl.semaphore_wait(barrier, n_chips + N_COL)

    def remote(src, dst, send, recv, device):
        return pltpu.make_async_remote_copy(
            src_ref=src, dst_ref=dst, send_sem=send, recv_sem=recv, device_id=device, device_id_type=MESH,
        )

    def unknowns(h, row):
        return x[h].at[pl.ds(OWN * row, OWN)]

    def gathers(h):
        return [
            remote(unknowns(h, row), unknowns(h, row), g_send.at[h, d], g_recv.at[h, d], (2 * peer + core, col))
            for d, peer in enumerate(to_chips)
        ]

    def relays(h, which=range(len(steps) + 1)):
        rows = [2 * peer + core for peer in from_chips] + [row]
        return [
            remote(unknowns(h, rows[d]), unknowns(h, rows[d]), y_send.at[h, d], y_recv.at[h, d], (other, col))
            for d in which
        ]

    def spreads(h):
        return [
            remote(part.at[h, peer], part_in.at[h, d], s_send.at[h, d], s_recv.at[h, d], (row, peer))
            for d, peer in enumerate(col_peers)
        ]

    def returns(h):
        mine = faces[h].at[pl.ds(FACES * col, FACES)]
        return [
            remote(mine, mine, a_send.at[h, d], a_recv.at[h, d], (row, peer)) for d, peer in enumerate(col_peers)
        ]

    def lends(h):
        return [remote(lent.at[h], lent_in.at[h], q_send.at[h], q_recv.at[h], (other, col))]

    def scatters(h):
        return [
            remote(middle.at[h, peer], middle_in.at[h, d], r_send.at[h, d], r_recv.at[h, d], (2 * peer + core, col))
            for d, peer in enumerate(to_chips)
        ]

    def start(copies):
        for copy in copies:
            copy.start()

    def arrived(copies):
        for copy in copies:
            copy.wait_recv()

    def left(copies):
        for copy in copies:
            copy.wait_send()

    def turn(n, values, turned):
        def body(step, carry):
            for u in range(8):
                turned[step * 8 + u] = values[step * 8 + u].T
            return carry

        lax.fori_loop(0, n // 8, body, 0)

    def sweep(which, n, values, source, sums):
        def body(step, total):
            products = []
            for u in range(UNROLL):
                at = step * UNROLL + u
                products.append(jnp.dot(
                    source[ints[3 * which + 1, at]], values[ints[3 * which, at]], preferred_element_type=F32
                ))
            for u in range(UNROLL):
                at = step * UNROLL + u
                total = total * floats[2 * which, at] + products[u]
                sums[at] = total
            return total

        if compute:
            lax.fori_loop(0, n // UNROLL, body, jnp.zeros((height, BLOCK), F32))

    def picked(which, sums, target):
        return sums[ints[3 * which + 2, target]] * floats[2 * which + 1, target]

    def forward(app, h):
        arrived(relays(h))
        if app == 0 and h == 0:
            load2.wait()
        sweep(FA, NB1, b1_turned, x[h], sums_a)
        sweep(FC, NB2, b2, x[h], sums_c)

        def hand_faces(m, carry):
            part[h, m, 0] = picked(FA, sums_a, m).astype(BF16)
            for b in range(FACES - 1):
                part[h, m, 1 + b] = picked(FC, sums_c, m * (FACES - 1) + b).astype(BF16)
            return carry

        lax.fori_loop(0, N_COL, hand_faces, 0)
        start(spreads(h))
        left(gathers(h) + relays(h))
        if app == 0 and h == 0:
            turn(NB2, b2, b2_turned)

    def sum_faces(app, h):
        arrived(spreads(h))

        def body(b, carry):
            total = part[h, col, b].astype(F32)
            for d in range(N_COL - 1):
                total = total + part_in[h, d, b].astype(F32)
            faces[h][col * FACES + b] = total.astype(BF16)
            return carry

        lax.fori_loop(0, FACES, body, 0)
        start(returns(h))

    def backward(app, h):
        arrived(returns(h))
        sweep(BA, NB1, b1, faces[h], sums_a)
        sweep(BC, NB2, b2_turned, faces[h], sums_c)

        def hand_image(m, carry):
            for b in range(OWN):
                t = (2 * m + 1 - core) * OWN + b
                lent[h, m, b] = (picked(BA, sums_a, t) + picked(BC, sums_c, t)).astype(BF16)
            return carry

        def keep_image(m, carry):
            for b in range(OWN):
                t = (2 * m + core) * OWN + b
                kept[h, m, b] = picked(BA, sums_a, t) + picked(BC, sums_c, t)
            return carry

        lax.fori_loop(0, N_ROW // 2, hand_image, 0)
        start(lends(h))
        lax.fori_loop(0, N_ROW // 2, keep_image, 0)
        left(spreads(h) + returns(h))

    def sum_cores(app, h):
        arrived(lends(h))

        def body(m, carry):
            for b in range(OWN):
                kept[h, m, b] = kept[h, m, b] + lent_in[h, m, b].astype(F32)
                middle[h, m, b] = kept[h, m, b].astype(BF16)
            return carry

        lax.fori_loop(0, N_ROW // 2, body, 0)
        start(scatters(h))

    def sum_chips(app, h):
        arrived(scatters(h))
        for b in range(OWN):
            total = kept[h, chip, b]
            for d in range(n_chips):
                total = total + middle_in[h, d, b].astype(F32)
            total = total * (1.0 / NORM)
            if app == apps - 1:
                out[b, h * height : (h + 1) * height, :] = total
            else:
                x[h][OWN * row + b] = total.astype(BF16)
        if app < apps - 1:
            begin(h)
        left(lends(h) + scatters(h))

    def begin(h):
        start(gathers(h) + relays(h, [n_chips]))

    def relay(app, h):
        for come, go in zip(gathers(h), relays(h, range(n_chips))):
            come.wait_recv()
            go.start()

    for h in range(parts):
        begin(h)
    load1.wait()
    turn(NB1, b1, b1_turned)
    run = {"Y": relay, "F": forward, "S": sum_faces, "B": backward, "Q": sum_cores, "R": sum_chips}
    for step, app, h in order or order_of(apps, parts):
        run[step](app, h)


def build(mesh, apps=APPS, parts=2, compute=True, order=None):
    tile = (K // parts, BLOCK)
    chips = N_ROW // 2

    def shards(vectors, b1_rows, b1_cols, b1_count, b1_values, b2_rows, b2_cols, b2_count, b2_values):
        counts = jnp.concatenate([b1_count[0], b2_count[0]])
        ints, floats = make_plans(counts, b1_rows[0], b1_cols[0], b2_rows[0], b2_cols[0])
        vmem = pl.BlockSpec(memory_space=pltpu.VMEM)
        smem = pl.BlockSpec(memory_space=pltpu.SMEM)
        hbm = pl.BlockSpec(memory_space=pl.ANY)
        dma = pltpu.SemaphoreType.DMA
        return pl.pallas_call(
            functools.partial(main_kernel, apps, parts, compute, order),
            out_shape=jax.ShapeDtypeStruct((OWN, K, BLOCK), F32),
            in_specs=[smem, smem, vmem, hbm, hbm],
            out_specs=vmem,
            scratch_shapes=[
                pltpu.VMEM((NB1, BLOCK, BLOCK), BF16),
                pltpu.VMEM((NB2, BLOCK, BLOCK), BF16),
                pltpu.VMEM((NB1, BLOCK, BLOCK), BF16),
                pltpu.VMEM((NB2, BLOCK, BLOCK), BF16),
                (pltpu.VMEM((EB_COL,) + tile, BF16),) * parts,
                pltpu.VMEM((NB2,) + tile, F32),
                pltpu.VMEM((NB1,) + tile, F32),
                pltpu.VMEM((parts, N_COL, FACES) + tile, BF16),
                pltpu.VMEM((parts, N_COL - 1, FACES) + tile, BF16),
                (pltpu.VMEM((N_COL * FACES,) + tile, BF16),) * parts,
                pltpu.VMEM((parts, chips, OWN) + tile, F32),
                pltpu.VMEM((parts, chips, OWN) + tile, BF16),
                pltpu.VMEM((parts, chips, OWN) + tile, BF16),
                pltpu.VMEM((parts, chips, OWN) + tile, BF16),
                pltpu.VMEM((parts, chips - 1, OWN) + tile, BF16),
                dma((2,)),
                dma((parts, chips - 1)), dma((parts, chips - 1)),
                dma((parts, chips)), dma((parts, chips)),
                dma((parts, N_COL - 1)), dma((parts, N_COL - 1)),
                dma((parts, N_COL - 1)), dma((parts, N_COL - 1)),
                dma((parts,)), dma((parts,)),
                dma((parts, chips - 1)), dma((parts, chips - 1)),
            ],
            compiler_params=pltpu.CompilerParams(
                collective_id=0, has_side_effects=True, vmem_limit_bytes=48 * 2**20
            ),
        )(ints, floats, vectors, b1_values[0, 0], b2_values[0, 0])

    return jax.shard_map(
        shards,
        mesh=mesh,
        in_specs=(
            P(("col", "row"), None, None),
            P("row", "col", None),
            P("row", "col", None),
            P("row", "col"),
            P("row", "col", None, None, None),
            P("row", "col", None),
            P("row", "col", None),
            P("row", "col"),
            P("row", "col", None, None, None),
        ),
        out_specs=P(("col", "row"), None, None),
        check_vma=False,
    )


def solution(mesh):
    return build(mesh)
```

```python
import functools

import jax
import jax.numpy as jnp
from jax import lax
from jax.experimental import pallas as pl
from jax.experimental.pallas import tpu as pltpu
from jax.sharding import PartitionSpec as P

BLOCK = 128
K = 64
APPS = 3
NB1 = 32
NB2 = 256
VB_ROW = 8
TB_ROW = 64
EB_COL = 32
NORM = 18432
N_ROW = 16
N_COL = 8
OWN = EB_COL // N_ROW
FACES = 1 + TB_ROW // N_COL
UNROLL = 64
MESH = pl.DeviceIdType.MESH
F32 = jnp.float32
BF16 = jnp.bfloat16

FC, FA, BC, BA = range(4)


def make_plans(count1, count2, rows1, cols1, rows2, cols2, ints, floats):
    def plan(which, target, source, filled, segments):
        n = target.shape[1]
        lanes = lax.broadcasted_iota(jnp.int32, (n, n), 1)
        rows = lax.broadcasted_iota(jnp.int32, (n, n), 0)
        place = lax.broadcasted_iota(jnp.int32, (1, n), 1)
        target = jnp.where(place < filled, target, segments)
        key = target * n + place

        def column(line):
            return jnp.sum(jnp.where(rows == lanes, line, 0), axis=1, keepdims=True)

        rank = jnp.sum(jnp.where(key < column(key), 1, 0), axis=1, keepdims=True)
        hit = rank == lanes
        follows = (rank + 1) == lanes

        def ordered(upright, mask):
            return jnp.sum(jnp.where(mask, upright, 0), axis=0, keepdims=True)

        upright = column(target)
        here = ordered(upright, hit)
        before = ordered(upright + 1, follows) - 1
        ints[3 * which : 3 * which + 1, :n] = ordered(rows, hit)
        ints[3 * which + 1 : 3 * which + 2, :n] = ordered(column(source), hit)
        floats[2 * which : 2 * which + 1, :n] = jnp.where(here == before, 1.0, 0.0)
        wide = 128
        segment = lax.broadcasted_iota(jnp.int32, (n, wide), 1)
        end = jnp.sum(jnp.where(upright <= segment, 1, 0), axis=0, keepdims=True)
        start = jnp.sum(jnp.where(upright < segment, 1, 0), axis=0, keepdims=True)
        ints[3 * which + 2 : 3 * which + 3, :wide] = jnp.maximum(end - 1, 0)
        floats[2 * which + 1 : 2 * which + 2, :wide] = jnp.where(end > start, 1.0, 0.0)

    ints[...] = jnp.zeros_like(ints)
    floats[...] = jnp.zeros_like(floats)
    per = TB_ROW // N_COL
    plan(FC, cols2, rows2, count2, TB_ROW)
    plan(FA, rows1, cols1, count1, VB_ROW)
    plan(BC, rows2, (cols2 // per) * FACES + 1 + cols2 % per, count2, EB_COL)
    plan(BA, cols1, rows1 * FACES, count1, EB_COL)


def main_kernel(
    apps, parts, compute,
    count1, count2, rows1_hbm, cols1_hbm, rows2_hbm, cols2_hbm, vectors, b1_hbm, b2_hbm, out,
    rows1, cols1, rows2, cols2, ints_vector, floats_vector, ints, floats,
    b1, b2, b1_turned, b2_turned, x, sums_c, sums_a, part, part_in, faces,
    kept, lent, lent_in, middle, middle_in,
    load_sem, g_send, g_recv, y_send, y_recv, s_send, s_recv, a_send, a_recv, q_send, q_recv, r_send, r_recv,
):
    row, col = lax.axis_index("row"), lax.axis_index("col")
    height = K // parts
    chip, core = row // 2, lax.rem(row, 2)
    z, xh = chip // 2, lax.rem(chip, 2)
    other = 2 * chip + 1 - core

    def chip_at(dz, dx):
        return lax.rem(z + dz, 4) * 2 + lax.rem(xh + dx, 2)

    steps = [(2, 1), (1, 1), (3, 1), (2, 0), (0, 1), (1, 0), (3, 0)]
    to_chips = [chip_at(dz, dx) for dz, dx in steps]
    from_chips = [chip_at(4 - dz, dx) for dz, dx in steps]
    xl, y = col // 4, lax.rem(col, 4)
    col_peers = [
        lax.rem(xl + dx, 2) * 4 + lax.rem(y + dy, 4) for dx, dy in [(1, 2), (1, 1), (1, 3), (0, 2), (1, 0), (0, 1), (0, 3)]
    ]
    n_chips = len(steps)

    def load(src, dst, at):
        copy = pltpu.make_async_copy(src, dst, load_sem.at[at])
        copy.start()
        return copy

    first = [
        load(vectors.at[:, pl.ds(h * height, height), :], x[h].at[pl.ds(OWN * row, OWN)], h) for h in range(parts)
    ]
    lists = [
        load(src, dst, parts + at)
        for at, (src, dst) in enumerate(
            [(rows1_hbm, rows1), (cols1_hbm, cols1), (rows2_hbm, rows2), (cols2_hbm, cols2)]
        )
    ]
    load1 = load(b1_hbm, b1, parts + 4)
    load2 = load(b2_hbm, b2, parts + 5)
    barrier = pltpu.get_barrier_semaphore()
    for peer in to_chips:
        pl.semaphore_signal(barrier, inc=1, device_id=(2 * peer + core, col), device_id_type=MESH)
    for peer in col_peers:
        pl.semaphore_signal(barrier, inc=1, device_id=(row, peer), device_id_type=MESH)
    pl.semaphore_signal(barrier, inc=1, device_id=(other, col), device_id_type=MESH)
    for copy in first:
        copy.wait()
    pl.semaphore_wait(barrier, n_chips + N_COL)

    def remote(src, dst, send, recv, device):
        return pltpu.make_async_remote_copy(
            src_ref=src, dst_ref=dst, send_sem=send, recv_sem=recv, device_id=device, device_id_type=MESH,
        )

    def unknowns(h, row):
        return x[h].at[pl.ds(OWN * row, OWN)]

    def gathers(h):
        return [
            remote(unknowns(h, row), unknowns(h, row), g_send.at[h, d], g_recv.at[h, d], (2 * peer + core, col))
            for d, peer in enumerate(to_chips)
        ]

    def relays(h, which=range(len(steps) + 1)):
        rows = [2 * peer + core for peer in from_chips] + [row]
        return [
            remote(unknowns(h, rows[d]), unknowns(h, rows[d]), y_send.at[h, d], y_recv.at[h, d], (other, col))
            for d in which
        ]

    def spreads(h):
        return [
            remote(part.at[h, peer], part_in.at[h, d], s_send.at[h, d], s_recv.at[h, d], (row, peer))
            for d, peer in enumerate(col_peers)
        ]

    def returns(h):
        mine = faces[h].at[pl.ds(FACES * col, FACES)]
        return [
            remote(mine, mine, a_send.at[h, d], a_recv.at[h, d], (row, peer)) for d, peer in enumerate(col_peers)
        ]

    def lends(h):
        return [remote(lent.at[h], lent_in.at[h], q_send.at[h], q_recv.at[h], (other, col))]

    def scatters(h):
        return [
            remote(middle.at[h, peer], middle_in.at[h, d], r_send.at[h, d], r_recv.at[h, d], (2 * peer + core, col))
            for d, peer in enumerate(to_chips)
        ]

    def start(copies):
        for copy in copies:
            copy.start()

    def arrived(copies):
        for copy in copies:
            copy.wait_recv()

    def left(copies):
        for copy in copies:
            copy.wait_send()

    def turn(n, values, turned):
        def body(step, carry):
            for u in range(8):
                turned[step * 8 + u] = values[step * 8 + u].T
            return carry

        lax.fori_loop(0, n // 8, body, 0)

    def sweep(which, n, values, source, sums):
        unroll = min(n, UNROLL)

        def body(step, total):
            products = []
            for u in range(0, unroll, 2):
                at = step * unroll + u
                blocks = [values[ints[3 * which, at + i]] for i in range(2)]
                picks = [source[ints[3 * which + 1, at + i]] for i in range(2)]
                both = jnp.dot(
                    jnp.concatenate(picks, axis=0), jnp.concatenate(blocks, axis=1), preferred_element_type=F32
                )
                products += [both[:height, :BLOCK], both[height:, BLOCK:]]
            for u in range(unroll):
                at = step * unroll + u
                total = total * floats[2 * which, at] + products[u]
                sums[at] = total
            return total

        if compute:
            lax.fori_loop(0, n // unroll, body, jnp.zeros((height, BLOCK), F32))

    def picked(which, sums, target):
        return sums[ints[3 * which + 2, target]] * floats[2 * which + 1, target]

    def forward(app, h):
        arrived(relays(h))
        sweep(FA, NB1, b1_turned, x[h], sums_a)
        sweep(FC, NB2, b2, x[h], sums_c)

        def hand_faces(m, carry):
            part[h, m, 0] = picked(FA, sums_a, m).astype(BF16)
            for b in range(FACES - 1):
                part[h, m, 1 + b] = picked(FC, sums_c, m * (FACES - 1) + b).astype(BF16)
            return carry

        lax.fori_loop(0, N_COL, hand_faces, 0)
        start(spreads(h))
        left(gathers(h) + relays(h))

        if h == 0:

            @pl.when(app == 0)
            def _():
                turn(NB2, b2, b2_turned)

    def sum_faces(app, h):
        arrived(spreads(h))

        def body(b, carry):
            total = part[h, col, b].astype(F32)
            for d in range(N_COL - 1):
                total = total + part_in[h, d, b].astype(F32)
            faces[h][col * FACES + b] = total.astype(BF16)
            return carry

        lax.fori_loop(0, FACES, body, 0)
        start(returns(h))

    def backward(app, h):
        arrived(returns(h))
        sweep(BA, NB1, b1, faces[h], sums_a)
        sweep(BC, NB2, b2_turned, faces[h], sums_c)

        def hand_image(m, carry):
            for b in range(OWN):
                t = (2 * m + 1 - core) * OWN + b
                lent[h, m, b] = (picked(BA, sums_a, t) + picked(BC, sums_c, t)).astype(BF16)
            return carry

        def keep_image(m, carry):
            for b in range(OWN):
                t = (2 * m + core) * OWN + b
                kept[h, m, b] = picked(BA, sums_a, t) + picked(BC, sums_c, t)
            return carry

        lax.fori_loop(0, N_ROW // 2, hand_image, 0)
        start(lends(h))
        lax.fori_loop(0, N_ROW // 2, keep_image, 0)
        left(spreads(h) + returns(h))

    def sum_cores(app, h):
        arrived(lends(h))

        def body(m, carry):
            for b in range(OWN):
                kept[h, m, b] = kept[h, m, b] + lent_in[h, m, b].astype(F32)
                middle[h, m, b] = kept[h, m, b].astype(BF16)
            return carry

        lax.fori_loop(0, N_ROW // 2, body, 0)
        start(scatters(h))

    def sum_chips(app, h):
        arrived(scatters(h))
        for b in range(OWN):
            total = kept[h, chip, b]
            for d in range(n_chips):
                total = total + middle_in[h, d, b].astype(F32)
            total = total * (1.0 / NORM)
            out[b, h * height : (h + 1) * height, :] = total
            x[h][OWN * row + b] = total.astype(BF16)

        @pl.when(app < apps - 1)
        def _():
            begin(h)

        left(lends(h) + scatters(h))

    def begin(h):
        start(gathers(h) + relays(h, [n_chips]))

    def relay(app, h):
        for come, go in zip(gathers(h), relays(h, range(n_chips))):
            come.wait_recv()
            go.start()

    for h in range(parts):
        begin(h)
    for copy in lists:
        copy.wait()
    make_plans(count1[0, 0], count2[0, 0], rows1[...], cols1[...], rows2[...], cols2[...], ints_vector, floats_vector)
    tables = [load(ints_vector, ints, parts + 6), load(floats_vector, floats, parts + 7)]
    load1.wait()
    turn(NB1, b1, b1_turned)
    for copy in tables:
        copy.wait()
    load2.wait()
    relay(0, 0)

    def application(app, carry):
        forward(app, 0)
        for h in range(1, parts):
            relay(app, h)
            forward(app, h)
        for h in range(parts):
            sum_faces(app, h)
        for h in range(parts):
            backward(app, h)
            sum_cores(app, h)
            if h:
                sum_chips(app, h - 1)

        @pl.when(app < apps - 1)
        def _():
            relay(app + 1, 0)

        sum_chips(app, parts - 1)
        return carry

    lax.fori_loop(0, apps, application, 0)


def build(mesh, apps=APPS, parts=2, compute=True):
    tile = (K // parts, BLOCK)
    chips = N_ROW // 2

    def shards(vectors, b1_rows, b1_cols, b1_count, b1_values, b2_rows, b2_cols, b2_count, b2_values):
        vmem = pl.BlockSpec(memory_space=pltpu.VMEM)
        smem = pl.BlockSpec(memory_space=pltpu.SMEM)
        hbm = pl.BlockSpec(memory_space=pl.ANY)
        dma = pltpu.SemaphoreType.DMA
        return pl.pallas_call(
            functools.partial(main_kernel, apps, parts, compute),
            out_shape=jax.ShapeDtypeStruct((OWN, K, BLOCK), F32),
            in_specs=[smem] * 2 + [hbm] * 7,
            out_specs=vmem,
            scratch_shapes=[
                pltpu.VMEM((1, NB1), jnp.int32),
                pltpu.VMEM((1, NB1), jnp.int32),
                pltpu.VMEM((1, NB2), jnp.int32),
                pltpu.VMEM((1, NB2), jnp.int32),
                pltpu.VMEM((16, NB2), jnp.int32),
                pltpu.VMEM((8, NB2), F32),
                pltpu.SMEM((16, NB2), jnp.int32),
                pltpu.SMEM((8, NB2), F32),
                pltpu.VMEM((NB1, BLOCK, BLOCK), BF16),
                pltpu.VMEM((NB2, BLOCK, BLOCK), BF16),
                pltpu.VMEM((NB1, BLOCK, BLOCK), BF16),
                pltpu.VMEM((NB2, BLOCK, BLOCK), BF16),
                (pltpu.VMEM((EB_COL,) + tile, BF16),) * parts,
                pltpu.VMEM((NB2,) + tile, F32),
                pltpu.VMEM((NB1,) + tile, F32),
                pltpu.VMEM((parts, N_COL, FACES) + tile, BF16),
                pltpu.VMEM((parts, N_COL - 1, FACES) + tile, BF16),
                (pltpu.VMEM((N_COL * FACES,) + tile, BF16),) * parts,
                pltpu.VMEM((parts, chips, OWN) + tile, F32),
                pltpu.VMEM((parts, chips, OWN) + tile, BF16),
                pltpu.VMEM((parts, chips, OWN) + tile, BF16),
                pltpu.VMEM((parts, chips, OWN) + tile, BF16),
                pltpu.VMEM((parts, chips - 1, OWN) + tile, BF16),
                dma((parts + 8,)),
                dma((parts, chips - 1)), dma((parts, chips - 1)),
                dma((parts, chips)), dma((parts, chips)),
                dma((parts, N_COL - 1)), dma((parts, N_COL - 1)),
                dma((parts, N_COL - 1)), dma((parts, N_COL - 1)),
                dma((parts,)), dma((parts,)),
                dma((parts, chips - 1)), dma((parts, chips - 1)),
            ],
            compiler_params=pltpu.CompilerParams(
                collective_id=0, has_side_effects=True, vmem_limit_bytes=60 * 2**20
            ),
        )(b1_count, b2_count, b1_rows[0], b1_cols[0], b2_rows[0], b2_cols[0], vectors, b1_values[0, 0], b2_values[0, 0])

    return jax.shard_map(
        shards,
        mesh=mesh,
        in_specs=(
            P(("col", "row"), None, None),
            P("row", "col", None),
            P("row", "col", None),
            P("row", "col"),
            P("row", "col", None, None, None),
            P("row", "col", None),
            P("row", "col", None),
            P("row", "col"),
            P("row", "col", None, None, None),
        ),
        out_specs=P(("col", "row"), None, None),
        check_vma=False,
    )


def solution(mesh):
    return build(mesh)
```

```python
import functools

import jax
import jax.numpy as jnp
from jax import lax
from jax.experimental import pallas as pl
from jax.experimental.pallas import tpu as pltpu
from jax.sharding import PartitionSpec as P

BLOCK = 128
K = 64
APPS = 3
NB1 = 32
NB2 = 256
VB_ROW = 8
TB_ROW = 64
EB_COL = 32
NORM = 18432
N_ROW = 16
N_COL = 8
OWN = EB_COL // N_ROW
FACES = 1 + TB_ROW // N_COL
SIDES = 2
RING = 4
FIRST = 4
SECOND = FACES - FIRST
UNROLL = 64
MESH = pl.DeviceIdType.MESH
F32 = jnp.float32
BF16 = jnp.bfloat16

FC, FA, BC, BA = range(4)


def make_plans(count1, count2, rows1, cols1, rows2, cols2, ints, floats):
    def plan(which, target, source, filled, segments):
        n = target.shape[1]
        lanes = lax.broadcasted_iota(jnp.int32, (n, n), 1)
        rows = lax.broadcasted_iota(jnp.int32, (n, n), 0)
        place = lax.broadcasted_iota(jnp.int32, (1, n), 1)
        target = jnp.where(place < filled, target, segments)
        key = target * n + place

        def column(line):
            return jnp.sum(jnp.where(rows == lanes, line, 0), axis=1, keepdims=True)

        rank = jnp.sum(jnp.where(key < column(key), 1, 0), axis=1, keepdims=True)
        hit = rank == lanes
        follows = (rank + 1) == lanes

        def ordered(upright, mask):
            return jnp.sum(jnp.where(mask, upright, 0), axis=0, keepdims=True)

        upright = column(target)
        here = ordered(upright, hit)
        before = ordered(upright + 1, follows) - 1
        ints[3 * which : 3 * which + 1, :n] = ordered(rows, hit)
        ints[3 * which + 1 : 3 * which + 2, :n] = ordered(column(source), hit)
        floats[2 * which : 2 * which + 1, :n] = jnp.where(here == before, 1.0, 0.0)
        wide = 128
        segment = lax.broadcasted_iota(jnp.int32, (n, wide), 1)
        end = jnp.sum(jnp.where(upright <= segment, 1, 0), axis=0, keepdims=True)
        start = jnp.sum(jnp.where(upright < segment, 1, 0), axis=0, keepdims=True)
        ints[3 * which + 2 : 3 * which + 3, :wide] = jnp.maximum(end - 1, 0)
        floats[2 * which + 1 : 2 * which + 2, :wide] = jnp.where(end > start, 1.0, 0.0)

    ints[...] = jnp.zeros_like(ints)
    floats[...] = jnp.zeros_like(floats)
    per = TB_ROW // N_COL

    def face_place(member, block):
        late = N_COL * FIRST + member * SECOND + block - FIRST
        return jnp.where(block < FIRST, member * FIRST + block, late)

    plan(FC, cols2, rows2, count2, TB_ROW)
    plan(FA, rows1, cols1, count1, VB_ROW)
    plan(BC, rows2, face_place(cols2 // per, 1 + cols2 % per), count2, EB_COL)
    plan(BA, cols1, rows1 * FIRST, count1, EB_COL)


def main_kernel(
    apps, parts, compute,
    count1, count2, rows1_hbm, cols1_hbm, rows2_hbm, cols2_hbm, vectors, b1_hbm, b2_hbm, out,
    rows1, cols1, rows2, cols2, ints_vector, floats_vector, ints, floats,
    b1, b2, b1_turned, b2_turned, x, sums_c, sums_a, part_p, part_q, p1_in, q1_in, mid_p, mid_q, own_q, p2_in, q2_in, faces,
    kept, lent, lent_in, middle, middle_in,
    load_sem, g_send, g_recv, y_send, y_recv, c_send, c_recv, q_send, q_recv, r_send, r_recv,
):
    row, col = lax.axis_index("row"), lax.axis_index("col")
    height = K // parts
    chip, core = row // 2, lax.rem(row, 2)
    z, xh = chip // 2, lax.rem(chip, 2)
    other = 2 * chip + 1 - core

    def chip_at(dz, dx):
        return lax.rem(z + dz, 4) * 2 + lax.rem(xh + dx, 2)

    steps = [(2, 1), (1, 1), (3, 1), (2, 0), (0, 1), (1, 0), (3, 0)]
    to_chips = [chip_at(dz, dx) for dz, dx in steps]
    from_chips = [chip_at(4 - dz, dx) for dz, dx in steps]
    xl, y = col // 4, lax.rem(col, 4)
    across = (row, (1 - xl) * RING + y)
    ring_to = [lax.rem(y + dy, RING) for dy in (2, 1, 3)]
    ring_from = [lax.rem(y + RING - dy, RING) for dy in (2, 1, 3)]
    n_chips = len(steps)

    def load(src, dst, at):
        copy = pltpu.make_async_copy(src, dst, load_sem.at[at])
        copy.start()
        return copy

    first = [
        load(vectors.at[:, pl.ds(h * height, height), :], x[h].at[pl.ds(OWN * row, OWN)], h) for h in range(parts)
    ]
    lists = [
        load(src, dst, parts + at)
        for at, (src, dst) in enumerate(
            [(rows1_hbm, rows1), (cols1_hbm, cols1), (rows2_hbm, rows2), (cols2_hbm, cols2)]
        )
    ]
    load1 = load(b1_hbm, b1, parts + 4)
    load2 = load(b2_hbm, b2, parts + 5)
    barrier = pltpu.get_barrier_semaphore()
    for peer in to_chips:
        pl.semaphore_signal(barrier, inc=1, device_id=(2 * peer + core, col), device_id_type=MESH)
    for peer in [across] + [(row, xl * RING + to) for to in ring_to]:
        pl.semaphore_signal(barrier, inc=1, device_id=peer, device_id_type=MESH)
    pl.semaphore_signal(barrier, inc=1, device_id=(other, col), device_id_type=MESH)
    for copy in first:
        copy.wait()
    pl.semaphore_wait(barrier, n_chips + 1 + RING)

    def remote(src, dst, send, recv, device):
        return pltpu.make_async_remote_copy(
            src_ref=src, dst_ref=dst, send_sem=send, recv_sem=recv, device_id=device, device_id_type=MESH,
        )

    def unknowns(h, row):
        return x[h].at[pl.ds(OWN * row, OWN)]

    def gathers(h):
        return [
            remote(unknowns(h, row), unknowns(h, row), g_send.at[h, d], g_recv.at[h, d], (2 * peer + core, col))
            for d, peer in enumerate(to_chips)
        ]

    def relays(h, which=range(len(steps) + 1)):
        rows = [2 * peer + core for peer in from_chips] + [row]
        return [
            remote(unknowns(h, rows[d]), unknowns(h, rows[d]), y_send.at[h, d], y_recv.at[h, d], (other, col))
            for d in which
        ]

    def hop(h, at, src, dst, device):
        return remote(src, dst, c_send.at[h, at], c_recv.at[h, at], device)

    def round_y(h, at, src_of, dst_of):
        return [
            hop(h, at + d, src_of(d, to), dst_of(d, to), (row, xl * RING + to)) for d, to in enumerate(ring_to)
        ]

    def firsts(h, start, count):
        return faces[h].at[pl.ds(start * FIRST, count * FIRST)]

    def seconds(h, member):
        return faces[h].at[pl.ds(N_COL * FIRST + member * SECOND, SECOND)]

    def across_p(h):
        return [hop(h, 0, part_p.at[h, 1 - xl], p1_in.at[h], across)]

    def around_q(h):
        return round_y(h, 1, lambda d, to: part_q.at[h, :, to], lambda d, to: q1_in.at[h, d])

    def around_p(h):
        return round_y(h, 4, lambda d, to: mid_p.at[h, to], lambda d, to: p2_in.at[h, d])

    def across_q(h):
        return [hop(h, 7, mid_q.at[h], q2_in.at[h], across)]

    def back_around_p(h):
        mine = firsts(h, col, 1)
        return round_y(h, 8, lambda d, to: mine, lambda d, to: mine)

    def back_around_q(h):
        mine = seconds(h, col)
        return round_y(h, 11, lambda d, to: mine, lambda d, to: mine)

    def back_across_q(h):
        mine = seconds(h, col)
        return [hop(h, 14, mine, mine, across)]

    def back_across_p(h):
        side = firsts(h, xl * RING, RING)
        return [hop(h, 15, side, side, across)]

    def back_around_again(h):
        theirs = seconds(h, (1 - xl) * RING + y)
        return round_y(h, 16, lambda d, to: theirs, lambda d, to: theirs)

    def lends(h):
        return [remote(lent.at[h], lent_in.at[h], q_send.at[h], q_recv.at[h], (other, col))]

    def scatters(h):
        return [
            remote(middle.at[h, peer], middle_in.at[h, d], r_send.at[h, d], r_recv.at[h, d], (2 * peer + core, col))
            for d, peer in enumerate(to_chips)
        ]

    def start(copies):
        for copy in copies:
            copy.start()

    def arrived(copies):
        for copy in copies:
            copy.wait_recv()

    def left(copies):
        for copy in copies:
            copy.wait_send()

    def turn(n, values, turned):
        def body(step, carry):
            for u in range(8):
                turned[step * 8 + u] = values[step * 8 + u].T
            return carry

        lax.fori_loop(0, n // 8, body, 0)

    def sweep(which, n, values, source, sums):
        unroll = min(n, UNROLL)

        def body(step, total):
            products = []
            for u in range(0, unroll, 2):
                at = step * unroll + u
                blocks = [values[ints[3 * which, at + i]] for i in range(2)]
                picks = [source[ints[3 * which + 1, at + i]] for i in range(2)]
                both = jnp.dot(
                    jnp.concatenate(picks, axis=0), jnp.concatenate(blocks, axis=1), preferred_element_type=F32
                )
                products += [both[:height, :BLOCK], both[height:, BLOCK:]]
            for u in range(unroll):
                at = step * unroll + u
                total = total * floats[2 * which, at] + products[u]
                sums[at] = total
            return total

        if compute:
            lax.fori_loop(0, n // unroll, body, jnp.zeros((height, BLOCK), F32))

    def picked(which, sums, target):
        return sums[ints[3 * which + 2, target]] * floats[2 * which + 1, target]

    def forward(app, h):
        arrived(relays(h))
        sweep(FA, NB1, b1_turned, x[h], sums_a)
        sweep(FC, NB2, b2, x[h], sums_c)

        def hand_faces(m, carry):
            side, at = m // RING, lax.rem(m, RING)
            part_p[h, side, at, 0] = picked(FA, sums_a, m).astype(BF16)
            for b in range(1, FIRST):
                part_p[h, side, at, b] = picked(FC, sums_c, m * (FACES - 1) + b - 1).astype(BF16)
            for b in range(SECOND):
                part_q[h, side, at, b] = picked(FC, sums_c, m * (FACES - 1) + FIRST + b - 1).astype(BF16)
            return carry

        lax.fori_loop(0, N_COL, hand_faces, 0)
        start(across_p(h) + around_q(h))
        left(gathers(h) + relays(h))


    def sum_pair(app, h):
        arrived(across_p(h))

        def body(to, carry):
            for b in range(FIRST):
                mid_p[h, to, b] = (part_p[h, xl, to, b].astype(F32) + p1_in[h, to, b].astype(F32)).astype(BF16)
            return carry

        lax.fori_loop(0, RING, body, 0)
        start(around_p(h))

    def sum_ring(app, h):
        arrived(around_q(h))
        for b in range(SECOND):
            own = part_q[h, xl, y, b].astype(F32)
            lent_sum = part_q[h, 1 - xl, y, b].astype(F32)
            for d in range(RING - 1):
                own = own + q1_in[h, d, xl, b].astype(F32)
                lent_sum = lent_sum + q1_in[h, d, 1 - xl, b].astype(F32)
            own_q[h, b] = own
            mid_q[h, b] = lent_sum.astype(BF16)
        start(across_q(h))

    def sum_faces(app, h):
        arrived(around_p(h) + across_q(h))
        for b in range(SECOND):
            faces[h][N_COL * FIRST + col * SECOND + b] = (own_q[h, b] + q2_in[h, b].astype(F32)).astype(BF16)
        start(back_across_q(h))
        for b in range(FIRST):
            total = mid_p[h, y, b].astype(F32)
            for d in range(RING - 1):
                total = total + p2_in[h, d, b].astype(F32)
            faces[h][col * FIRST + b] = total.astype(BF16)
        start(back_around_p(h) + back_around_q(h))

    def pass_on(app, h):
        arrived(back_across_q(h))
        start(back_around_again(h))
        arrived(back_around_p(h))
        start(back_across_p(h))

    def backward(app, h):
        arrived(back_around_q(h) + back_around_again(h) + back_across_p(h))
        sweep(BA, NB1, b1, faces[h], sums_a)
        sweep(BC, NB2, b2_turned, faces[h], sums_c)

        def hand_image(m, carry):
            for b in range(OWN):
                t = (2 * m + 1 - core) * OWN + b
                lent[h, m, b] = (picked(BA, sums_a, t) + picked(BC, sums_c, t)).astype(BF16)
            return carry

        def keep_image(m, carry):
            for b in range(OWN):
                t = (2 * m + core) * OWN + b
                kept[h, m, b] = picked(BA, sums_a, t) + picked(BC, sums_c, t)
            return carry

        lax.fori_loop(0, N_ROW // 2, hand_image, 0)
        start(lends(h))
        lax.fori_loop(0, N_ROW // 2, keep_image, 0)
        left(across_p(h) + around_q(h) + around_p(h) + across_q(h) + back_around_p(h) + back_around_q(h))
        left(back_across_q(h) + back_across_p(h) + back_around_again(h))

    def sum_cores(app, h):
        arrived(lends(h))

        def body(m, carry):
            for b in range(OWN):
                kept[h, m, b] = kept[h, m, b] + lent_in[h, m, b].astype(F32)
                middle[h, m, b] = kept[h, m, b].astype(BF16)
            return carry

        lax.fori_loop(0, N_ROW // 2, body, 0)
        start(scatters(h))

    def sum_chips(app, h):
        arrived(scatters(h))
        for b in range(OWN):
            total = kept[h, chip, b]
            for d in range(n_chips):
                total = total + middle_in[h, d, b].astype(F32)
            total = total * (1.0 / NORM)
            out[b, h * height : (h + 1) * height, :] = total
            x[h][OWN * row + b] = total.astype(BF16)

        @pl.when(app < apps - 1)
        def _():
            begin(h)

        left(lends(h) + scatters(h))

    def begin(h):
        start(gathers(h) + relays(h, [n_chips]))

    def relay(app, h):
        for come, go in zip(gathers(h), relays(h, range(n_chips))):
            come.wait_recv()
            go.start()

    for h in range(parts):
        begin(h)
    for copy in lists:
        copy.wait()
    make_plans(count1[0, 0], count2[0, 0], rows1[...], cols1[...], rows2[...], cols2[...], ints_vector, floats_vector)
    tables = [load(ints_vector, ints, parts + 6), load(floats_vector, floats, parts + 7)]
    load1.wait()
    turn(NB1, b1, b1_turned)
    relay(0, 0)
    for copy in tables:
        copy.wait()
    load2.wait()

    def application(app, carry):
        forward(app, 0)
        for h in range(1, parts):
            relay(app, h)
            forward(app, h)

        @pl.when(app == 0)
        def _():
            turn(NB2, b2, b2_turned)

        for h in range(parts):
            sum_pair(app, h)
            sum_ring(app, h)
        for h in range(parts):
            sum_faces(app, h)
        for h in range(parts):
            pass_on(app, h)
        for h in range(parts):
            backward(app, h)
            sum_cores(app, h)
            if h:
                sum_chips(app, h - 1)

        @pl.when(app < apps - 1)
        def _():
            relay(app + 1, 0)

        sum_chips(app, parts - 1)
        return carry

    lax.fori_loop(0, apps, application, 0)


def build(mesh, apps=APPS, parts=2, compute=True):
    tile = (K // parts, BLOCK)
    chips = N_ROW // 2

    def shards(vectors, b1_rows, b1_cols, b1_count, b1_values, b2_rows, b2_cols, b2_count, b2_values):
        vmem = pl.BlockSpec(memory_space=pltpu.VMEM)
        smem = pl.BlockSpec(memory_space=pltpu.SMEM)
        hbm = pl.BlockSpec(memory_space=pl.ANY)
        dma = pltpu.SemaphoreType.DMA
        return pl.pallas_call(
            functools.partial(main_kernel, apps, parts, compute),
            out_shape=jax.ShapeDtypeStruct((OWN, K, BLOCK), F32),
            in_specs=[smem] * 2 + [hbm] * 7,
            out_specs=vmem,
            scratch_shapes=[
                pltpu.VMEM((1, NB1), jnp.int32),
                pltpu.VMEM((1, NB1), jnp.int32),
                pltpu.VMEM((1, NB2), jnp.int32),
                pltpu.VMEM((1, NB2), jnp.int32),
                pltpu.VMEM((16, NB2), jnp.int32),
                pltpu.VMEM((8, NB2), F32),
                pltpu.SMEM((16, NB2), jnp.int32),
                pltpu.SMEM((8, NB2), F32),
                pltpu.VMEM((NB1, BLOCK, BLOCK), BF16),
                pltpu.VMEM((NB2, BLOCK, BLOCK), BF16),
                pltpu.VMEM((NB1, BLOCK, BLOCK), BF16),
                pltpu.VMEM((NB2, BLOCK, BLOCK), BF16),
                (pltpu.VMEM((EB_COL,) + tile, BF16),) * parts,
                pltpu.VMEM((NB2,) + tile, F32),
                pltpu.VMEM((NB1,) + tile, F32),
                pltpu.VMEM((parts, SIDES, RING, FIRST) + tile, BF16),
                pltpu.VMEM((parts, SIDES, RING, SECOND) + tile, BF16),
                pltpu.VMEM((parts, RING, FIRST) + tile, BF16),
                pltpu.VMEM((parts, RING - 1, SIDES, SECOND) + tile, BF16),
                pltpu.VMEM((parts, RING, FIRST) + tile, BF16),
                pltpu.VMEM((parts, SECOND) + tile, BF16),
                pltpu.VMEM((parts, SECOND) + tile, F32),
                pltpu.VMEM((parts, RING - 1, FIRST) + tile, BF16),
                pltpu.VMEM((parts, SECOND) + tile, BF16),
                (pltpu.VMEM((N_COL * FACES,) + tile, BF16),) * parts,
                pltpu.VMEM((parts, chips, OWN) + tile, F32),
                pltpu.VMEM((parts, chips, OWN) + tile, BF16),
                pltpu.VMEM((parts, chips, OWN) + tile, BF16),
                pltpu.VMEM((parts, chips, OWN) + tile, BF16),
                pltpu.VMEM((parts, chips - 1, OWN) + tile, BF16),
                dma((parts + 8,)),
                dma((parts, chips - 1)), dma((parts, chips - 1)),
                dma((parts, chips)), dma((parts, chips)),
                dma((parts, 19)), dma((parts, 19)),
                dma((parts,)), dma((parts,)),
                dma((parts, chips - 1)), dma((parts, chips - 1)),
            ],
            compiler_params=pltpu.CompilerParams(
                collective_id=0, has_side_effects=True, vmem_limit_bytes=60 * 2**20
            ),
        )(b1_count, b2_count, b1_rows[0], b1_cols[0], b2_rows[0], b2_cols[0], vectors, b1_values[0, 0], b2_values[0, 0])

    return jax.shard_map(
        shards,
        mesh=mesh,
        in_specs=(
            P(("col", "row"), None, None),
            P("row", "col", None),
            P("row", "col", None),
            P("row", "col"),
            P("row", "col", None, None, None),
            P("row", "col", None),
            P("row", "col", None),
            P("row", "col"),
            P("row", "col", None, None, None),
        ),
        out_specs=P(("col", "row"), None, None),
        check_vma=False,
    )


def solution(mesh):
    return build(mesh)
```

```python
import functools

import jax
import jax.numpy as jnp
from jax import lax
from jax.experimental import pallas as pl
from jax.experimental.pallas import tpu as pltpu
from jax.sharding import PartitionSpec as P

BLOCK = 128
K = 64
APPS = 3
NB1 = 32
NB2 = 256
VB_ROW = 8
TB_ROW = 64
EB_COL = 32
NORM = 18432
N_ROW = 16
N_COL = 8
OWN = EB_COL // N_ROW
FACES = 1 + TB_ROW // N_COL
SIDES = 2
RING = 4
FIRST = 4
SECOND = FACES - FIRST
UNROLL = 128
MESH = pl.DeviceIdType.MESH
F32 = jnp.float32
BF16 = jnp.bfloat16

FC, FA, BC, BA = range(4)


def make_plans(count1, count2, rows1, cols1, rows2, cols2, ints, floats):
    def plan(which, target, source, filled, segments):
        n = target.shape[1]
        lanes = lax.broadcasted_iota(jnp.int32, (n, n), 1)
        rows = lax.broadcasted_iota(jnp.int32, (n, n), 0)
        place = lax.broadcasted_iota(jnp.int32, (1, n), 1)
        target = jnp.where(place < filled, target, segments)
        key = target * n + place

        def column(line):
            return jnp.sum(jnp.where(rows == lanes, line, 0), axis=1, keepdims=True)

        rank = jnp.sum(jnp.where(key < column(key), 1, 0), axis=1, keepdims=True)
        hit = rank == lanes
        follows = (rank + 1) == lanes

        def ordered(upright, mask):
            return jnp.sum(jnp.where(mask, upright, 0), axis=0, keepdims=True)

        upright = column(target)
        here = ordered(upright, hit)
        before = ordered(upright + 1, follows) - 1
        ints[3 * which : 3 * which + 1, :n] = ordered(rows, hit)
        ints[3 * which + 1 : 3 * which + 2, :n] = ordered(column(source), hit)
        floats[2 * which : 2 * which + 1, :n] = jnp.where(here == before, 1.0, 0.0)
        wide = 128
        segment = lax.broadcasted_iota(jnp.int32, (n, wide), 1)
        end = jnp.sum(jnp.where(upright <= segment, 1, 0), axis=0, keepdims=True)
        start = jnp.sum(jnp.where(upright < segment, 1, 0), axis=0, keepdims=True)
        ints[3 * which + 2 : 3 * which + 3, :wide] = jnp.maximum(end - 1, 0)
        floats[2 * which + 1 : 2 * which + 2, :wide] = jnp.where(end > start, 1.0, 0.0)

    ints[...] = jnp.zeros_like(ints)
    floats[...] = jnp.zeros_like(floats)
    per = TB_ROW // N_COL

    def face_place(member, block):
        late = N_COL * FIRST + member * SECOND + block - FIRST
        return jnp.where(block < FIRST, member * FIRST + block, late)

    plan(FC, cols2, rows2, count2, TB_ROW)
    plan(FA, rows1, cols1, count1, VB_ROW)
    plan(BC, rows2, face_place(cols2 // per, 1 + cols2 % per), count2, EB_COL)
    plan(BA, cols1, rows1 * FIRST, count1, EB_COL)


def main_kernel(
    apps, parts,
    count1, count2, rows1_hbm, cols1_hbm, rows2_hbm, cols2_hbm, vectors, b1_hbm, b2_hbm, out,
    rows1, cols1, rows2, cols2, ints_vector, floats_vector, ints, floats,
    b1, b2, b1_turned, b2_turned, x, sums_c, sums_a, part_p, part_q, p1_in, q1_in, mid_p, mid_q, own_q, p2_in, q2_in, faces,
    kept, lent, lent_in, middle, middle_in,
    load_sem, g_send, g_recv, y_send, y_recv, c_send, c_recv, q_send, q_recv, r_send, r_recv,
):
    row, col = lax.axis_index("row"), lax.axis_index("col")
    height = K // parts
    chip, core = row // 2, lax.rem(row, 2)
    z, xh = chip // 2, lax.rem(chip, 2)
    other = 2 * chip + 1 - core

    def chip_at(dz, dx):
        return lax.rem(z + dz, 4) * 2 + lax.rem(xh + dx, 2)

    steps = [(2, 1), (1, 1), (3, 1), (2, 0), (0, 1), (1, 0), (3, 0)]
    to_chips = [chip_at(dz, dx) for dz, dx in steps]
    from_chips = [chip_at(4 - dz, dx) for dz, dx in steps]
    xl, y = col // 4, lax.rem(col, 4)
    across = (row, (1 - xl) * RING + y)
    ring_to = [lax.rem(y + dy, RING) for dy in (2, 1, 3)]
    ring_from = [lax.rem(y + RING - dy, RING) for dy in (2, 1, 3)]
    n_chips = len(steps)

    def load(src, dst, at):
        copy = pltpu.make_async_copy(src, dst, load_sem.at[at])
        copy.start()
        return copy

    first = [
        load(vectors.at[:, pl.ds(h * height, height), :], x[h].at[pl.ds(OWN * row, OWN)], h) for h in range(parts)
    ]
    lists = [
        load(src, dst, parts + at)
        for at, (src, dst) in enumerate(
            [(rows1_hbm, rows1), (cols1_hbm, cols1), (rows2_hbm, rows2), (cols2_hbm, cols2)]
        )
    ]
    load1 = load(b1_hbm, b1, parts + 4)
    load2 = load(b2_hbm, b2, parts + 5)
    barrier = pltpu.get_barrier_semaphore()
    for peer in to_chips:
        pl.semaphore_signal(barrier, inc=1, device_id=(2 * peer + core, col), device_id_type=MESH)
    for peer in [across] + [(row, xl * RING + to) for to in ring_to]:
        pl.semaphore_signal(barrier, inc=1, device_id=peer, device_id_type=MESH)
    pl.semaphore_signal(barrier, inc=1, device_id=(other, col), device_id_type=MESH)
    for copy in first:
        copy.wait()
    pl.semaphore_wait(barrier, n_chips + 1 + RING)

    def remote(src, dst, send, recv, device):
        return pltpu.make_async_remote_copy(
            src_ref=src, dst_ref=dst, send_sem=send, recv_sem=recv, device_id=device, device_id_type=MESH,
        )

    def unknowns(h, row):
        return x[h].at[pl.ds(OWN * row, OWN)]

    def gathers(h):
        return [
            remote(unknowns(h, row), unknowns(h, row), g_send.at[h, d], g_recv.at[h, d], (2 * peer + core, col))
            for d, peer in enumerate(to_chips)
        ]

    def relays(h, which=range(len(steps) + 1)):
        rows = [2 * peer + core for peer in from_chips] + [row]
        return [
            remote(unknowns(h, rows[d]), unknowns(h, rows[d]), y_send.at[h, d], y_recv.at[h, d], (other, col))
            for d in which
        ]

    def hop(h, at, src, dst, device):
        return remote(src, dst, c_send.at[h, at], c_recv.at[h, at], device)

    def round_y(h, at, src_of, dst_of):
        return [
            hop(h, at + d, src_of(d, to), dst_of(d, to), (row, xl * RING + to)) for d, to in enumerate(ring_to)
        ]

    def firsts(h, start, count):
        return faces[h].at[pl.ds(start * FIRST, count * FIRST)]

    def seconds(h, member):
        return faces[h].at[pl.ds(N_COL * FIRST + member * SECOND, SECOND)]

    def across_p(h):
        return [hop(h, 0, part_p.at[h, 1 - xl], p1_in.at[h], across)]

    def around_q(h):
        return round_y(h, 1, lambda d, to: part_q.at[h, :, to], lambda d, to: q1_in.at[h, d])

    def around_p(h):
        return round_y(h, 4, lambda d, to: mid_p.at[h, to], lambda d, to: p2_in.at[h, d])

    def across_q(h):
        return [hop(h, 7, mid_q.at[h], q2_in.at[h], across)]

    def back_around_p(h):
        mine = firsts(h, col, 1)
        return round_y(h, 8, lambda d, to: mine, lambda d, to: mine)

    def back_around_q(h):
        mine = seconds(h, col)
        return round_y(h, 11, lambda d, to: mine, lambda d, to: mine)

    def back_across_q(h):
        mine = seconds(h, col)
        return [hop(h, 14, mine, mine, across)]

    def back_across_p(h):
        side = firsts(h, xl * RING, RING)
        return [hop(h, 15, side, side, across)]

    def back_around_again(h):
        theirs = seconds(h, (1 - xl) * RING + y)
        return round_y(h, 16, lambda d, to: theirs, lambda d, to: theirs)

    def lends(h):
        return [remote(lent.at[h], lent_in.at[h], q_send.at[h], q_recv.at[h], (other, col))]

    def scatters(h):
        return [
            remote(middle.at[h, peer], middle_in.at[h, d], r_send.at[h, d], r_recv.at[h, d], (2 * peer + core, col))
            for d, peer in enumerate(to_chips)
        ]

    def start(copies):
        for copy in copies:
            copy.start()

    def arrived(copies):
        for copy in copies:
            copy.wait_recv()

    def left(copies):
        for copy in copies:
            copy.wait_send()

    def turn(n, values, turned):
        def body(step, carry):
            for u in range(8):
                turned[step * 8 + u] = values[step * 8 + u].T
            return carry

        lax.fori_loop(0, n // 8, body, 0)

    def sweep(which, n, values, source, sums):
        unroll = min(n, UNROLL)

        def body(step, total):
            products = []
            for u in range(0, unroll, 2):
                at = step * unroll + u
                blocks = [values[ints[3 * which, at + i]] for i in range(2)]
                picks = [source[ints[3 * which + 1, at + i]] for i in range(2)]
                both = jnp.dot(
                    jnp.concatenate(picks, axis=0), jnp.concatenate(blocks, axis=1), preferred_element_type=F32
                )
                products += [both[:height, :BLOCK], both[height:, BLOCK:]]
            for u in range(unroll):
                at = step * unroll + u
                total = total * floats[2 * which, at] + products[u]
                sums[at] = total
            return total

        if n == unroll:
            body(0, jnp.zeros((height, BLOCK), F32))
        else:
            lax.fori_loop(0, n // unroll, body, jnp.zeros((height, BLOCK), F32))

    def picked(which, sums, target):
        return sums[ints[3 * which + 2, target]] * floats[2 * which + 1, target]

    def forward(app, h):
        arrived(relays(h))
        sweep(FA, NB1, b1_turned, x[h], sums_a)
        sweep(FC, NB2, b2, x[h], sums_c)

        def hand_faces(m, carry):
            side, at = m // RING, lax.rem(m, RING)
            part_p[h, side, at, 0] = picked(FA, sums_a, m).astype(BF16)
            for b in range(1, FIRST):
                part_p[h, side, at, b] = picked(FC, sums_c, m * (FACES - 1) + b - 1).astype(BF16)
            for b in range(SECOND):
                part_q[h, side, at, b] = picked(FC, sums_c, m * (FACES - 1) + FIRST + b - 1).astype(BF16)
            return carry

        lax.fori_loop(0, N_COL, hand_faces, 0)
        start(across_p(h) + around_q(h))
        left(gathers(h) + relays(h))


    def sum_pair(app, h):
        arrived(across_p(h))

        def body(to, carry):
            for b in range(FIRST):
                mid_p[h, to, b] = (part_p[h, xl, to, b].astype(F32) + p1_in[h, to, b].astype(F32)).astype(BF16)
            return carry

        lax.fori_loop(0, RING, body, 0)
        start(around_p(h))

    def sum_ring(app, h):
        arrived(around_q(h))
        for b in range(SECOND):
            own = part_q[h, xl, y, b].astype(F32)
            lent_sum = part_q[h, 1 - xl, y, b].astype(F32)
            for d in range(RING - 1):
                own = own + q1_in[h, d, xl, b].astype(F32)
                lent_sum = lent_sum + q1_in[h, d, 1 - xl, b].astype(F32)
            own_q[h, b] = own
            mid_q[h, b] = lent_sum.astype(BF16)
        start(across_q(h))

    def sum_faces(app, h):
        arrived(around_p(h) + across_q(h))
        for b in range(SECOND):
            faces[h][N_COL * FIRST + col * SECOND + b] = (own_q[h, b] + q2_in[h, b].astype(F32)).astype(BF16)
        start(back_across_q(h))
        for b in range(FIRST):
            total = mid_p[h, y, b].astype(F32)
            for d in range(RING - 1):
                total = total + p2_in[h, d, b].astype(F32)
            faces[h][col * FIRST + b] = total.astype(BF16)
        start(back_around_p(h) + back_around_q(h))

    def pass_on(app, h):
        arrived(back_across_q(h))
        start(back_around_again(h))
        arrived(back_around_p(h))
        start(back_across_p(h))

    def backward(app, h):
        arrived(back_around_q(h) + back_around_again(h) + back_across_p(h))
        sweep(BA, NB1, b1, faces[h], sums_a)
        sweep(BC, NB2, b2_turned, faces[h], sums_c)

        def hand_image(m, carry):
            for b in range(OWN):
                t = (2 * m + 1 - core) * OWN + b
                lent[h, m, b] = (picked(BA, sums_a, t) + picked(BC, sums_c, t)).astype(BF16)
            return carry

        def keep_image(m, carry):
            for b in range(OWN):
                t = (2 * m + core) * OWN + b
                kept[h, m, b] = picked(BA, sums_a, t) + picked(BC, sums_c, t)
            return carry

        lax.fori_loop(0, N_ROW // 2, hand_image, 0)
        start(lends(h))
        lax.fori_loop(0, N_ROW // 2, keep_image, 0)
        left(across_p(h) + around_q(h) + around_p(h) + across_q(h) + back_around_p(h) + back_around_q(h))
        left(back_across_q(h) + back_across_p(h) + back_around_again(h))

    def sum_cores(app, h):
        arrived(lends(h))

        def body(m, carry):
            for b in range(OWN):
                kept[h, m, b] = kept[h, m, b] + lent_in[h, m, b].astype(F32)
                middle[h, m, b] = kept[h, m, b].astype(BF16)
            return carry

        lax.fori_loop(0, N_ROW // 2, body, 0)
        start(scatters(h))

    def sum_chips(app, h):
        arrived(scatters(h))
        for b in range(OWN):
            total = kept[h, chip, b]
            for d in range(n_chips):
                total = total + middle_in[h, d, b].astype(F32)
            total = total * (1.0 / NORM)
            out[b, h * height : (h + 1) * height, :] = total
            x[h][OWN * row + b] = total.astype(BF16)

        @pl.when(app < apps - 1)
        def _():
            begin(h)

        left(lends(h) + scatters(h))

    def begin(h):
        start(gathers(h) + relays(h, [n_chips]))

    def relay(app, h):
        for come, go in zip(gathers(h), relays(h, range(n_chips))):
            come.wait_recv()
            go.start()

    for h in range(parts):
        begin(h)
    for copy in lists:
        copy.wait()
    make_plans(count1[0, 0], count2[0, 0], rows1[...], cols1[...], rows2[...], cols2[...], ints_vector, floats_vector)
    tables = [load(ints_vector, ints, parts + 6), load(floats_vector, floats, parts + 7)]
    load1.wait()
    turn(NB1, b1, b1_turned)
    relay(0, 0)
    for copy in tables:
        copy.wait()
    load2.wait()

    def application(app, carry):
        forward(app, 0)
        for h in range(1, parts):
            relay(app, h)
            forward(app, h)

        @pl.when(app == 0)
        def _():
            turn(NB2, b2, b2_turned)

        for h in range(parts):
            sum_pair(app, h)
            sum_ring(app, h)
        for h in range(parts):
            sum_faces(app, h)
        for h in range(parts):
            pass_on(app, h)
        for h in range(parts):
            backward(app, h)
            sum_cores(app, h)
            if h:
                sum_chips(app, h - 1)

        @pl.when(app < apps - 1)
        def _():
            relay(app + 1, 0)

        sum_chips(app, parts - 1)
        return carry

    lax.fori_loop(0, apps, application, 0)


def build(mesh, apps=APPS, parts=2):
    tile = (K // parts, BLOCK)
    chips = N_ROW // 2

    def shards(vectors, b1_rows, b1_cols, b1_count, b1_values, b2_rows, b2_cols, b2_count, b2_values):
        vmem = pl.BlockSpec(memory_space=pltpu.VMEM)
        smem = pl.BlockSpec(memory_space=pltpu.SMEM)
        hbm = pl.BlockSpec(memory_space=pl.ANY)
        dma = pltpu.SemaphoreType.DMA
        return pl.pallas_call(
            functools.partial(main_kernel, apps, parts),
            out_shape=jax.ShapeDtypeStruct((OWN, K, BLOCK), F32),
            in_specs=[smem] * 2 + [hbm] * 7,
            out_specs=vmem,
            scratch_shapes=[
                pltpu.VMEM((1, NB1), jnp.int32),
                pltpu.VMEM((1, NB1), jnp.int32),
                pltpu.VMEM((1, NB2), jnp.int32),
                pltpu.VMEM((1, NB2), jnp.int32),
                pltpu.VMEM((16, NB2), jnp.int32),
                pltpu.VMEM((8, NB2), F32),
                pltpu.SMEM((16, NB2), jnp.int32),
                pltpu.SMEM((8, NB2), F32),
                pltpu.VMEM((NB1, BLOCK, BLOCK), BF16),
                pltpu.VMEM((NB2, BLOCK, BLOCK), BF16),
                pltpu.VMEM((NB1, BLOCK, BLOCK), BF16),
                pltpu.VMEM((NB2, BLOCK, BLOCK), BF16),
                (pltpu.VMEM((EB_COL,) + tile, BF16),) * parts,
                pltpu.VMEM((NB2,) + tile, F32),
                pltpu.VMEM((NB1,) + tile, F32),
                pltpu.VMEM((parts, SIDES, RING, FIRST) + tile, BF16),
                pltpu.VMEM((parts, SIDES, RING, SECOND) + tile, BF16),
                pltpu.VMEM((parts, RING, FIRST) + tile, BF16),
                pltpu.VMEM((parts, RING - 1, SIDES, SECOND) + tile, BF16),
                pltpu.VMEM((parts, RING, FIRST) + tile, BF16),
                pltpu.VMEM((parts, SECOND) + tile, BF16),
                pltpu.VMEM((parts, SECOND) + tile, F32),
                pltpu.VMEM((parts, RING - 1, FIRST) + tile, BF16),
                pltpu.VMEM((parts, SECOND) + tile, BF16),
                (pltpu.VMEM((N_COL * FACES,) + tile, BF16),) * parts,
                pltpu.VMEM((parts, chips, OWN) + tile, F32),
                pltpu.VMEM((parts, chips, OWN) + tile, BF16),
                pltpu.VMEM((parts, chips, OWN) + tile, BF16),
                pltpu.VMEM((parts, chips, OWN) + tile, BF16),
                pltpu.VMEM((parts, chips - 1, OWN) + tile, BF16),
                dma((parts + 8,)),
                dma((parts, chips - 1)), dma((parts, chips - 1)),
                dma((parts, chips)), dma((parts, chips)),
                dma((parts, 19)), dma((parts, 19)),
                dma((parts,)), dma((parts,)),
                dma((parts, chips - 1)), dma((parts, chips - 1)),
            ],
            compiler_params=pltpu.CompilerParams(
                collective_id=0, has_side_effects=True, vmem_limit_bytes=60 * 2**20
            ),
        )(b1_count, b2_count, b1_rows[0], b1_cols[0], b2_rows[0], b2_cols[0], vectors, b1_values[0, 0], b2_values[0, 0])

    return jax.shard_map(
        shards,
        mesh=mesh,
        in_specs=(
            P(("col", "row"), None, None),
            P("row", "col", None),
            P("row", "col", None),
            P("row", "col"),
            P("row", "col", None, None, None),
            P("row", "col", None),
            P("row", "col", None),
            P("row", "col"),
            P("row", "col", None, None, None),
        ),
        out_specs=P(("col", "row"), None, None),
        check_vma=False,
    )


def solution(mesh):
    return build(mesh)
```

```python
import functools

import jax
import jax.numpy as jnp
from jax import lax
from jax.experimental import pallas as pl
from jax.experimental.pallas import tpu as pltpu
from jax.sharding import PartitionSpec as P

BLOCK = 128
K = 64
APPS = 3
NB1 = 32
NB2 = 256
VB_ROW = 8
TB_ROW = 64
EB_COL = 32
NORM = 18432
N_ROW = 16
N_COL = 8
OWN = EB_COL // N_ROW
FACES = 1 + TB_ROW // N_COL
SIDES = 2
RING = 4
FIRST = 4
SECOND = FACES - FIRST
UNROLL = 128
MESH = pl.DeviceIdType.MESH
F32 = jnp.float32
BF16 = jnp.bfloat16

FC, FA, BC, BA = range(4)


def make_plans(count1, count2, rows1, cols1, rows2, cols2, ints, floats):
    def plan(which, target, source, filled, segments):
        n = target.shape[1]
        lanes = lax.broadcasted_iota(jnp.int32, (n, n), 1)
        rows = lax.broadcasted_iota(jnp.int32, (n, n), 0)
        place = lax.broadcasted_iota(jnp.int32, (1, n), 1)
        target = jnp.where(place < filled, target, segments)
        key = target * n + place

        def column(line):
            return jnp.sum(jnp.where(rows == lanes, line, 0), axis=1, keepdims=True)

        rank = jnp.sum(jnp.where(key < column(key), 1, 0), axis=1, keepdims=True)
        hit = rank == lanes
        follows = (rank + 1) == lanes

        def ordered(upright, mask):
            return jnp.sum(jnp.where(mask, upright, 0), axis=0, keepdims=True)

        upright = column(target)
        here = ordered(upright, hit)
        before = ordered(upright + 1, follows) - 1
        ints[3 * which : 3 * which + 1, :n] = ordered(rows, hit)
        ints[3 * which + 1 : 3 * which + 2, :n] = ordered(column(source), hit)
        floats[2 * which : 2 * which + 1, :n] = jnp.where(here == before, 1.0, 0.0)
        wide = 128
        segment = lax.broadcasted_iota(jnp.int32, (n, wide), 1)
        end = jnp.sum(jnp.where(upright <= segment, 1, 0), axis=0, keepdims=True)
        start = jnp.sum(jnp.where(upright < segment, 1, 0), axis=0, keepdims=True)
        ints[3 * which + 2 : 3 * which + 3, :wide] = jnp.maximum(end - 1, 0)
        floats[2 * which + 1 : 2 * which + 2, :wide] = jnp.where(end > start, 1.0, 0.0)

    ints[...] = jnp.zeros_like(ints)
    floats[...] = jnp.zeros_like(floats)
    per = TB_ROW // N_COL

    def face_place(member, block):
        late = N_COL * FIRST + member * SECOND + block - FIRST
        return jnp.where(block < FIRST, member * FIRST + block, late)

    plan(FC, cols2, rows2, count2, TB_ROW)
    plan(FA, rows1, cols1, count1, VB_ROW)
    plan(BC, rows2, face_place(cols2 // per, 1 + cols2 % per), count2, EB_COL)
    plan(BA, cols1, rows1 * FIRST, count1, EB_COL)


def main_kernel(
    apps, parts,
    count1, count2, rows1_hbm, cols1_hbm, rows2_hbm, cols2_hbm, vectors, b1_hbm, b2_hbm, out,
    rows1, cols1, rows2, cols2, ints_vector, floats_vector, ints, floats,
    b1, b2, b1_turned, b2_turned, x, sums_c, sums_a, part_p, part_q, p1_in, q1_in, mid_p, mid_q, own_q, p2_in, q2_in, faces,
    kept, lent, lent_in, middle, middle_in,
    load_sem, g_send, g_recv, y_send, y_recv, c_send, c_recv, q_send, q_recv, r_send, r_recv,
):
    row, col = lax.axis_index("row"), lax.axis_index("col")
    height = K // parts
    chip, core = row // 2, lax.rem(row, 2)
    z, xh = chip // 2, lax.rem(chip, 2)
    other = 2 * chip + 1 - core

    def chip_at(dz, dx):
        return lax.rem(z + dz, 4) * 2 + lax.rem(xh + dx, 2)

    steps = [(2, 1), (1, 1), (3, 1), (2, 0), (0, 1), (1, 0), (3, 0)]
    to_chips = [chip_at(dz, dx) for dz, dx in steps]
    from_chips = [chip_at(4 - dz, dx) for dz, dx in steps]
    xl, y = col // 4, lax.rem(col, 4)
    across = (row, (1 - xl) * RING + y)
    ring_to = [lax.rem(y + dy, RING) for dy in (2, 1, 3)]
    ring_from = [lax.rem(y + RING - dy, RING) for dy in (2, 1, 3)]
    n_chips = len(steps)

    def load(src, dst, at):
        copy = pltpu.make_async_copy(src, dst, load_sem.at[at])
        copy.start()
        return copy

    first = [
        load(vectors.at[:, pl.ds(h * height, height), :], x[h].at[pl.ds(OWN * row, OWN)], h) for h in range(parts)
    ]
    lists = [
        load(src, dst, parts + at)
        for at, (src, dst) in enumerate(
            [(rows1_hbm, rows1), (cols1_hbm, cols1), (rows2_hbm, rows2), (cols2_hbm, cols2)]
        )
    ]
    load1 = load(b1_hbm, b1, parts + 4)
    load2 = load(b2_hbm, b2, parts + 5)
    barrier = pltpu.get_barrier_semaphore()
    for peer in to_chips:
        pl.semaphore_signal(barrier, inc=1, device_id=(2 * peer + core, col), device_id_type=MESH)
    for peer in [across] + [(row, xl * RING + to) for to in ring_to]:
        pl.semaphore_signal(barrier, inc=1, device_id=peer, device_id_type=MESH)
    pl.semaphore_signal(barrier, inc=1, device_id=(other, col), device_id_type=MESH)
    for copy in first:
        copy.wait()
    pl.semaphore_wait(barrier, n_chips + 1 + RING)

    def remote(src, dst, send, recv, device):
        return pltpu.make_async_remote_copy(
            src_ref=src, dst_ref=dst, send_sem=send, recv_sem=recv, device_id=device, device_id_type=MESH,
        )

    def unknowns(h, row):
        return x[h].at[pl.ds(OWN * row, OWN)]

    def gathers(h):
        return [
            remote(unknowns(h, row), unknowns(h, row), g_send.at[h, d], g_recv.at[h, d], (2 * peer + core, col))
            for d, peer in enumerate(to_chips)
        ]

    def relays(h, which=range(len(steps) + 1)):
        rows = [2 * peer + core for peer in from_chips] + [row]
        return [
            remote(unknowns(h, rows[d]), unknowns(h, rows[d]), y_send.at[h, d], y_recv.at[h, d], (other, col))
            for d in which
        ]

    def hop(h, at, src, dst, device):
        return remote(src, dst, c_send.at[h, at], c_recv.at[h, at], device)

    def round_y(h, at, src_of, dst_of):
        return [
            hop(h, at + d, src_of(d, to), dst_of(d, to), (row, xl * RING + to)) for d, to in enumerate(ring_to)
        ]

    def firsts(h, start, count):
        return faces[h].at[pl.ds(start * FIRST, count * FIRST)]

    def seconds(h, member):
        return faces[h].at[pl.ds(N_COL * FIRST + member * SECOND, SECOND)]

    def across_p(h):
        return [hop(h, 0, part_p.at[h, 1 - xl], p1_in.at[h], across)]

    def around_q(h):
        return round_y(h, 1, lambda d, to: part_q.at[h, :, to], lambda d, to: q1_in.at[h, d])

    def around_p(h):
        return round_y(h, 4, lambda d, to: mid_p.at[h, to], lambda d, to: p2_in.at[h, d])

    def across_q(h):
        return [hop(h, 7, mid_q.at[h], q2_in.at[h], across)]

    def back_around_p(h):
        mine = firsts(h, col, 1)
        return round_y(h, 8, lambda d, to: mine, lambda d, to: mine)

    def back_around_q(h):
        mine = seconds(h, col)
        return round_y(h, 11, lambda d, to: mine, lambda d, to: mine)

    def back_across_q(h):
        mine = seconds(h, col)
        return [hop(h, 14, mine, mine, across)]

    def back_across_p(h):
        side = firsts(h, xl * RING, RING)
        return [hop(h, 15, side, side, across)]

    def back_around_again(h):
        theirs = seconds(h, (1 - xl) * RING + y)
        return round_y(h, 16, lambda d, to: theirs, lambda d, to: theirs)

    def lends(h):
        return [remote(lent.at[h], lent_in.at[h], q_send.at[h], q_recv.at[h], (other, col))]

    def scatters(h):
        return [
            remote(middle.at[h, peer], middle_in.at[h, d], r_send.at[h, d], r_recv.at[h, d], (2 * peer + core, col))
            for d, peer in enumerate(to_chips)
        ]

    def start(copies):
        for copy in copies:
            copy.start()

    def arrived(copies):
        for copy in copies:
            copy.wait_recv()

    def left(copies):
        for copy in copies:
            copy.wait_send()

    def turn(n, values, turned):
        def body(step, carry):
            for u in range(8):
                turned[step * 8 + u] = values[step * 8 + u].T
            return carry

        lax.fori_loop(0, n // 8, body, 0)

    def sweep(which, n, values, source, sums):
        unroll = min(n, UNROLL)

        def body(step, total):
            products = []
            for u in range(0, unroll, 2):
                at = step * unroll + u
                blocks = [values[ints[3 * which, at + i]] for i in range(2)]
                picks = [source[ints[3 * which + 1, at + i]] for i in range(2)]
                both = jnp.dot(
                    jnp.concatenate(picks, axis=0), jnp.concatenate(blocks, axis=1), preferred_element_type=F32
                )
                products += [both[:height, :BLOCK], both[height:, BLOCK:]]
            for u in range(unroll):
                at = step * unroll + u
                total = total * floats[2 * which, at] + products[u]
                sums[at] = total
            return total

        if n == unroll:
            body(0, jnp.zeros((height, BLOCK), F32))
        else:
            lax.fori_loop(0, n // unroll, body, jnp.zeros((height, BLOCK), F32))

    def picked(which, sums, target):
        return sums[ints[3 * which + 2, target]] * floats[2 * which + 1, target]

    def forward(app, h):
        arrived(relays(h))
        sweep(FA, NB1, b1_turned, x[h], sums_a)
        sweep(FC, NB2, b2, x[h], sums_c)

        def hand_faces(m, carry):
            side, at = m // RING, lax.rem(m, RING)
            part_p[h, side, at, 0] = picked(FA, sums_a, m).astype(BF16)
            for b in range(1, FIRST):
                part_p[h, side, at, b] = picked(FC, sums_c, m * (FACES - 1) + b - 1).astype(BF16)
            for b in range(SECOND):
                part_q[h, side, at, b] = picked(FC, sums_c, m * (FACES - 1) + FIRST + b - 1).astype(BF16)
            return carry

        lax.fori_loop(0, N_COL, hand_faces, 0)
        start(across_p(h) + around_q(h))
        left(gathers(h) + relays(h))


    def sum_pair(app, h):
        arrived(across_p(h))

        def body(to, carry):
            for b in range(FIRST):
                mid_p[h, to, b] = (part_p[h, xl, to, b].astype(F32) + p1_in[h, to, b].astype(F32)).astype(BF16)
            return carry

        lax.fori_loop(0, RING, body, 0)
        start(around_p(h))

    def sum_ring(app, h):
        arrived(around_q(h))
        for b in range(SECOND):
            own = part_q[h, xl, y, b].astype(F32)
            lent_sum = part_q[h, 1 - xl, y, b].astype(F32)
            for d in range(RING - 1):
                own = own + q1_in[h, d, xl, b].astype(F32)
                lent_sum = lent_sum + q1_in[h, d, 1 - xl, b].astype(F32)
            own_q[h, b] = own
            mid_q[h, b] = lent_sum.astype(BF16)
        start(across_q(h))

    def sum_faces(app, h):
        arrived(around_p(h) + across_q(h))
        for b in range(SECOND):
            faces[h][N_COL * FIRST + col * SECOND + b] = (own_q[h, b] + q2_in[h, b].astype(F32)).astype(BF16)
        start(back_across_q(h))
        for b in range(FIRST):
            total = mid_p[h, y, b].astype(F32)
            for d in range(RING - 1):
                total = total + p2_in[h, d, b].astype(F32)
            faces[h][col * FIRST + b] = total.astype(BF16)
        start(back_around_p(h) + back_around_q(h))

    def pass_on(app, h):
        arrived(back_across_q(h))
        start(back_around_again(h))
        arrived(back_around_p(h))
        start(back_across_p(h))

    def backward(app, h):
        arrived(back_around_q(h) + back_around_again(h) + back_across_p(h))
        sweep(BA, NB1, b1, faces[h], sums_a)
        sweep(BC, NB2, b2_turned, faces[h], sums_c)

        def hand_image(m, carry):
            for b in range(OWN):
                t = (2 * m + 1 - core) * OWN + b
                lent[h, m, b] = (picked(BA, sums_a, t) + picked(BC, sums_c, t)).astype(BF16)
            return carry

        def keep_image(m, carry):
            for b in range(OWN):
                t = (2 * m + core) * OWN + b
                kept[h, m, b] = picked(BA, sums_a, t) + picked(BC, sums_c, t)
            return carry

        lax.fori_loop(0, N_ROW // 2, hand_image, 0)
        start(lends(h))
        lax.fori_loop(0, N_ROW // 2, keep_image, 0)
        left(across_p(h) + around_q(h) + around_p(h) + across_q(h) + back_around_p(h) + back_around_q(h))
        left(back_across_q(h) + back_across_p(h) + back_around_again(h))

    def sum_cores(app, h):
        arrived(lends(h))

        def body(m, carry):
            for b in range(OWN):
                kept[h, m, b] = kept[h, m, b] + lent_in[h, m, b].astype(F32)
                middle[h, m, b] = kept[h, m, b].astype(BF16)
            return carry

        lax.fori_loop(0, N_ROW // 2, body, 0)
        start(scatters(h))

    def sum_chips(app, h):
        arrived(scatters(h))
        for b in range(OWN):
            total = kept[h, chip, b]
            for d in range(n_chips):
                total = total + middle_in[h, d, b].astype(F32)
            total = total * (1.0 / NORM)
            out[b, h * height : (h + 1) * height, :] = total
            x[h][OWN * row + b] = total.astype(BF16)

        @pl.when(app < apps - 1)
        def _():
            begin(h)

        left(lends(h) + scatters(h))

    def begin(h):
        start(gathers(h) + relays(h, [n_chips]))

    def relay(app, h):
        for come, go in zip(gathers(h), relays(h, range(n_chips))):
            come.wait_recv()
            go.start()

    for h in range(parts):
        begin(h)
    for copy in lists:
        copy.wait()
    make_plans(count1[0, 0], count2[0, 0], rows1[...], cols1[...], rows2[...], cols2[...], ints_vector, floats_vector)
    tables = [load(ints_vector, ints, parts + 6), load(floats_vector, floats, parts + 7)]
    load1.wait()
    turn(NB1, b1, b1_turned)
    relay(0, 0)
    for copy in tables:
        copy.wait()
    load2.wait()

    def faces_of(app, h, inner):
        forward(app, h)
        inner[0]()
        sum_pair(app, h)
        sum_ring(app, h)
        inner[1]()
        sum_faces(app, h)
        pass_on(app, h)

    def image_of(app, h):
        backward(app, h)
        sum_cores(app, h)

    forward(0, 0)
    turn(NB2, b2, b2_turned)
    for step in (sum_pair, sum_ring, sum_faces, pass_on):
        step(0, 0)
    relay(0, 1)

    def application(app, carry):
        more = pl.when(app < apps - 1)
        faces_of(app, 1, (lambda: image_of(app, 0), lambda: sum_chips(app, 0)))

        @more
        def _():
            relay(app + 1, 0)
            forward(app + 1, 0)

        image_of(app, 1)

        @more
        def _():
            sum_pair(app + 1, 0)
            sum_ring(app + 1, 0)

        sum_chips(app, 1)

        @more
        def _():
            sum_faces(app + 1, 0)
            pass_on(app + 1, 0)
            relay(app + 1, 1)

        return carry

    lax.fori_loop(0, apps, application, 0)


def build(mesh, apps=APPS, parts=2):
    tile = (K // parts, BLOCK)
    chips = N_ROW // 2

    def shards(vectors, b1_rows, b1_cols, b1_count, b1_values, b2_rows, b2_cols, b2_count, b2_values):
        vmem = pl.BlockSpec(memory_space=pltpu.VMEM)
        smem = pl.BlockSpec(memory_space=pltpu.SMEM)
        hbm = pl.BlockSpec(memory_space=pl.ANY)
        dma = pltpu.SemaphoreType.DMA
        return pl.pallas_call(
            functools.partial(main_kernel, apps, parts),
            out_shape=jax.ShapeDtypeStruct((OWN, K, BLOCK), F32),
            in_specs=[smem] * 2 + [hbm] * 7,
            out_specs=vmem,
            scratch_shapes=[
                pltpu.VMEM((1, NB1), jnp.int32),
                pltpu.VMEM((1, NB1), jnp.int32),
                pltpu.VMEM((1, NB2), jnp.int32),
                pltpu.VMEM((1, NB2), jnp.int32),
                pltpu.VMEM((16, NB2), jnp.int32),
                pltpu.VMEM((8, NB2), F32),
                pltpu.SMEM((16, NB2), jnp.int32),
                pltpu.SMEM((8, NB2), F32),
                pltpu.VMEM((NB1, BLOCK, BLOCK), BF16),
                pltpu.VMEM((NB2, BLOCK, BLOCK), BF16),
                pltpu.VMEM((NB1, BLOCK, BLOCK), BF16),
                pltpu.VMEM((NB2, BLOCK, BLOCK), BF16),
                (pltpu.VMEM((EB_COL,) + tile, BF16),) * parts,
                pltpu.VMEM((NB2,) + tile, F32),
                pltpu.VMEM((NB1,) + tile, F32),
                pltpu.VMEM((parts, SIDES, RING, FIRST) + tile, BF16),
                pltpu.VMEM((parts, SIDES, RING, SECOND) + tile, BF16),
                pltpu.VMEM((parts, RING, FIRST) + tile, BF16),
                pltpu.VMEM((parts, RING - 1, SIDES, SECOND) + tile, BF16),
                pltpu.VMEM((parts, RING, FIRST) + tile, BF16),
                pltpu.VMEM((parts, SECOND) + tile, BF16),
                pltpu.VMEM((parts, SECOND) + tile, F32),
                pltpu.VMEM((parts, RING - 1, FIRST) + tile, BF16),
                pltpu.VMEM((parts, SECOND) + tile, BF16),
                (pltpu.VMEM((N_COL * FACES,) + tile, BF16),) * parts,
                pltpu.VMEM((parts, chips, OWN) + tile, F32),
                pltpu.VMEM((parts, chips, OWN) + tile, BF16),
                pltpu.VMEM((parts, chips, OWN) + tile, BF16),
                pltpu.VMEM((parts, chips, OWN) + tile, BF16),
                pltpu.VMEM((parts, chips - 1, OWN) + tile, BF16),
                dma((parts + 8,)),
                dma((parts, chips - 1)), dma((parts, chips - 1)),
                dma((parts, chips)), dma((parts, chips)),
                dma((parts, 19)), dma((parts, 19)),
                dma((parts,)), dma((parts,)),
                dma((parts, chips - 1)), dma((parts, chips - 1)),
            ],
            compiler_params=pltpu.CompilerParams(
                collective_id=0, has_side_effects=True, vmem_limit_bytes=60 * 2**20
            ),
        )(b1_count, b2_count, b1_rows[0], b1_cols[0], b2_rows[0], b2_cols[0], vectors, b1_values[0, 0], b2_values[0, 0])

    return jax.shard_map(
        shards,
        mesh=mesh,
        in_specs=(
            P(("col", "row"), None, None),
            P("row", "col", None),
            P("row", "col", None),
            P("row", "col"),
            P("row", "col", None, None, None),
            P("row", "col", None),
            P("row", "col", None),
            P("row", "col"),
            P("row", "col", None, None, None),
        ),
        out_specs=P(("col", "row"), None, None),
        check_vma=False,
    )


def solution(mesh):
    return build(mesh)
```
